32 devices in a mesh: groups: 2 (over y), row: 4 (over z), col: 4 (over x, core).
Axes of the slice: x: 2, y: 2, z: 4, core: 2. Of those that a mesh axis runs over, the one named last changes fastest.
Arguments:
- tokens: bfloat16 [256, 4096], P(('groups', 'row'), 'col'), parts along dimension 0, may hold values from -6 to 6
- out_grad: bfloat16 [256, 4096], P(('groups', 'row'), 'col'), parts along dimension 0, may hold values from -6 to 6
- gate_weight: bfloat16 [8192, 14336], P(('groups', 'col'), 'row'), parts along dimension 0, may hold values from -0.1875 to 0.1875
- up_weight: bfloat16 [8192, 14336], P(('groups', 'col'), 'row'), parts along dimension 0, may hold values from -0.1875 to 0.1875
- down_weight: bfloat16 [28672, 4096], P(('groups', 'row'), 'col'), parts along dimension 0, may hold values from -0.09375 to 0.09375
- gate_mask: int32 [64, 112], P('groups'), parts along dimension 0, may hold values 0 or 1
- up_mask: int32 [64, 112], P('groups'), parts along dimension 0, may hold values 0 or 1
- down_mask: int32 [224, 32], P('groups'), parts along dimension 0, may hold values 0 or 1
Outputs:
- grad_tokens: bfloat16 [256, 4096], P(('groups', 'row'), 'col'), parts along dimension 0
- grad_gate: bfloat16 [8192, 14336], P(('groups', 'col'), 'row'), parts along dimension 0
- grad_up: bfloat16 [8192, 14336], P(('groups', 'col'), 'row'), parts along dimension 0
- grad_down: bfloat16 [28672, 4096], P(('groups', 'row'), 'col'), parts along dimension 0
The draws below stay inside these ranges and needn't reach their ends.
There are 2 independent parts, one for each index of `groups`. The reference program is written for one: setup_inputs(seed, part) draws one part's arguments, and reference() takes and returns one part's arrays. A program takes and returns all parts, laid end to end along the dimension named above; each array names one. Nothing has to cross between parts.
All inputs are finite; a program needn't handle non-finite values.
Results may differ from the reference program's by a relative error of at most 0.019.
Values may be sent and summed in bfloat16 or wider, within the bound.
No kernel may reach another device: no remote copies, remote signals or barrier semaphores. Data moves between devices by JAX's collectives and lax.ppermute only.
A program may use at most 128 MiB of HBM per device.

```python
import jax
import jax.numpy as jnp
from jax import lax

D = 4096
FF = 14336
BLK = 128
TOKENS = 128
N_ROW = 4
N_COL = 4


def touch_ends(result, rng, least, largest):
    dims = result.shape
    place = [jax.random.randint(jax.random.fold_in(rng, axis), (), 0, dims[axis]) for axis in range(len(dims))]
    result = result.at[tuple(place)].set(least)
    longest = dims.index(max(dims))
    place[longest] = (place[longest] + 1) % dims[longest]
    return result.at[tuple(place)].set(largest)


def steps_of(rng, shape, cuts, low, high):
    def one(position, blocks):
        draws = jax.random.uniform(jax.random.fold_in(jax.random.fold_in(rng, 6), position), (blocks,), jnp.float32, low / len(cuts), high / len(cuts))
        return jnp.repeat(jnp.exp(draws), shape[position] // blocks).reshape((-1,) + (1,) * (len(shape) - position - 1))

    factor_of = one(*cuts[0])
    for cut in cuts[1:]:
        factor_of = factor_of * one(*cut)
    return factor_of


def normal_values(key, extent, scale, limit, cuts=(), kind=jnp.bfloat16):
    drawn = scale * jax.random.normal(key, extent, jnp.float32)
    if cuts:
        drawn = drawn * steps_of(key, extent, cuts, -0.22, 0.18)
    return jnp.clip(drawn, -limit, limit).astype(kind)


def setup_inputs(seed: int = 0, part: int = 0) -> dict:
    splits = jax.random.split(jax.random.key(seed), 9)
    own_keys = jax.random.split(jax.random.fold_in(splits[8], part), 9)
    return {
        "tokens": normal_values(own_keys[0], (TOKENS, D), 1.0, 6.0, ((0, 4), (1, 4))),
        "out_grad": normal_values(own_keys[1], (TOKENS, D), 1.0, 6.0, ((0, 4), (1, 4))),
        "gate_weight": normal_values(own_keys[2], (D, FF), (D // 4) ** -0.5, 0.1875, ((0, 4), (1, 4))),
        "up_weight": normal_values(own_keys[3], (D, FF), (D // 4) ** -0.5, 0.1875, ((0, 4), (1, 4))),
        "down_weight": normal_values(own_keys[4], (FF, D), (FF // 4) ** -0.5, 0.09375, ((0, 4), (1, 4))),
        "gate_mask": touch_ends((jax.random.randint(own_keys[5], (D // BLK, FF // BLK), 0, 4) < 1).astype(jnp.int32), jax.random.fold_in(own_keys[5], 1), 0, 1),
        "up_mask": touch_ends((jax.random.randint(own_keys[6], (D // BLK, FF // BLK), 0, 4) < 1).astype(jnp.int32), jax.random.fold_in(own_keys[6], 1), 0, 1),
        "down_mask": touch_ends((jax.random.randint(own_keys[7], (FF // BLK, D // BLK), 0, 4) < 1).astype(jnp.int32), jax.random.fold_in(own_keys[7], 1), 0, 1),
    }


def masked(values, block_table):
    keep_cells = jnp.repeat(jnp.repeat(block_table > 0, BLK, axis=0), BLK, axis=1)
    return jnp.where(keep_cells, values, jnp.zeros((), values.dtype))


def blocked_product(left, right, pieces):
    width = left.shape[1] // pieces

    def step(total, index):
        start = index * width
        left_part = lax.dynamic_slice_in_dim(left, start, width, 1)
        right_part = lax.dynamic_slice_in_dim(right, start, width, 0)
        term = jnp.dot(left_part, right_part, preferred_element_type=jnp.float32).astype(jnp.bfloat16)
        term = lax.optimization_barrier(term)
        return total + term.astype(jnp.float32), None

    start_total = jnp.zeros((left.shape[0], right.shape[1]), jnp.float32)
    total, unused = lax.scan(step, start_total, jnp.arange(pieces, dtype=jnp.int32))
    return total


def blocked_pair(left_one, right_one, left_two, right_two, pieces):
    width = left_one.shape[1] // pieces

    def step(total, index):
        start = index * width
        term = (jnp.dot(lax.dynamic_slice_in_dim(left_one, start, width, 1),
                        lax.dynamic_slice_in_dim(right_one, start, width, 0), preferred_element_type=jnp.float32)
                + jnp.dot(lax.dynamic_slice_in_dim(left_two, start, width, 1),
                          lax.dynamic_slice_in_dim(right_two, start, width, 0), preferred_element_type=jnp.float32))
        term = lax.optimization_barrier(term.astype(jnp.bfloat16))
        return total + term.astype(jnp.float32), None

    start_total = jnp.zeros((left_one.shape[0], right_one.shape[1]), jnp.float32)
    total, unused = lax.scan(step, start_total, jnp.arange(pieces, dtype=jnp.int32))
    return total


def reference(tokens, out_grad, gate_weight, up_weight, down_weight, gate_mask, up_mask, down_mask):
    gate_live = masked(gate_weight, gate_mask)
    up_live = masked(up_weight, up_mask)
    down_live = masked(down_weight, down_mask)
    gate_pre = blocked_product(tokens, gate_live, N_COL)
    up_pre = blocked_product(tokens, up_live, N_COL)
    hidden_grad = blocked_product(out_grad, down_live.T, N_COL)
    sigmoid_gate = jax.nn.sigmoid(gate_pre)
    active = gate_pre * sigmoid_gate
    hidden = (active * up_pre).astype(jnp.bfloat16)
    grad_up_act = (hidden_grad * active).astype(jnp.bfloat16)
    grad_gate_act = (hidden_grad * up_pre * sigmoid_gate * (1.0 + gate_pre * (1.0 - sigmoid_gate))).astype(jnp.bfloat16)
    grad_tokens = blocked_pair(grad_gate_act, gate_live.T, grad_up_act, up_live.T, N_ROW).astype(jnp.bfloat16)
    grad_gate = masked(jnp.dot(tokens.T, grad_gate_act, preferred_element_type=jnp.float32), gate_mask).astype(jnp.bfloat16)
    grad_up = masked(jnp.dot(tokens.T, grad_up_act, preferred_element_type=jnp.float32), up_mask).astype(jnp.bfloat16)
    grad_down = masked(jnp.dot(hidden.T, out_grad, preferred_element_type=jnp.float32), down_mask).astype(jnp.bfloat16)
    return grad_tokens, grad_gate, grad_up, grad_down
```

```python
import functools

import jax
import jax.numpy as jnp
from jax import lax
from jax.experimental import pallas as pl
from jax.experimental.pallas import tpu as pltpu
from jax.sharding import PartitionSpec as P

BLK = 128
TILE = 512
VMEM_LIMIT = 40 * 1024 * 1024
BF = jnp.bfloat16
F32 = jnp.float32


def params():
    return pltpu.CompilerParams(vmem_limit_bytes=VMEM_LIMIT)


def gcd_of(a, b):
    while b:
        a, b = b, a % b
    return a


def block_index(first, count, step):
    return (first + jnp.arange(count, dtype=jnp.int32) * step) // BLK


def pick(table, row_index, col_index):
    rows = (row_index[:, None] == jnp.arange(table.shape[0], dtype=jnp.int32)[None, :]).astype(BF)
    cols = (jnp.arange(table.shape[1], dtype=jnp.int32)[:, None] == col_index[None, :]).astype(BF)
    part = jnp.dot(rows, (table > 0).astype(BF), preferred_element_type=F32).astype(BF)
    return jnp.dot(part, cols, preferred_element_type=F32).astype(BF)


def mask_rows(weight, keep, rows):
    return jnp.concatenate(
        [weight[i * rows : (i + 1) * rows, :] * keep[i : i + 1, :] for i in range(keep.shape[0])], axis=0
    )


def dot_nt(left, right):
    return lax.dot_general(left, right, (((1,), (1,)), ((), ())), preferred_element_type=F32)


def dot_tn(left, right):
    return lax.dot_general(left, right, (((0,), (0,)), ((), ())), preferred_element_type=F32)


def forward_kernel(x_ref, og_ref, gate_ref, up_ref, down_ref, gk_ref, uk_ref, dk_ref, keep_ref, send_ref):
    half = keep_ref.shape[1]
    granule = down_ref.shape[0] // dk_ref.shape[1]
    x = x_ref[...]
    gate = jnp.dot(x, mask_rows(gate_ref[...], gk_ref[...], BLK), preferred_element_type=F32).astype(BF)
    up = jnp.dot(x, mask_rows(up_ref[...], uk_ref[...], BLK), preferred_element_type=F32).astype(BF)
    grad = dot_nt(og_ref[...], mask_rows(down_ref[...], dk_ref[0], granule)).astype(BF)
    for i, part in enumerate((gate, up, grad)):
        keep_ref[i] = part[:half]
        send_ref[i] = part[half:]


def forward(x, og, gate_w, up_w, down_w, gk, uk, dk, first, tiles, tile):
    rows, feats = x.shape
    half = rows // 2
    span = tiles * tile
    out = jax.ShapeDtypeStruct((3, half, span), BF)
    return pl.pallas_call(
        forward_kernel,
        out_shape=(out, out),
        grid=(tiles,),
        in_specs=[
            pl.BlockSpec((rows, feats), lambda i: (0, 0)),
            pl.BlockSpec((rows, feats), lambda i: (0, 0)),
            pl.BlockSpec((feats, tile), lambda i: (0, first + i)),
            pl.BlockSpec((feats, tile), lambda i: (0, first + i)),
            pl.BlockSpec((tile, feats), lambda i: (first + i, 0)),
            pl.BlockSpec((gk.shape[0], tile), lambda i: (0, first + i)),
            pl.BlockSpec((uk.shape[0], tile), lambda i: (0, first + i)),
            pl.BlockSpec((1,) + dk.shape[1:], lambda i: (first + i, 0, 0)),
        ],
        out_specs=[pl.BlockSpec((3, half, tile), lambda i: (0, 0, i))] * 2,
        compiler_params=params(),
        cost_estimate=pl.CostEstimate(
            flops=6 * rows * feats * span, bytes_accessed=6 * feats * span + 4 * rows * feats, transcendentals=0
        ),
        name="forward",
    )(x, og, gate_w, up_w, down_w, gk, uk, dk)


def grad_tokens_kernel(n_parts, prev_ref, gate_ref, up_ref, gk_ref, uk_ref, *rest):
    parts, out_ref = rest[:n_parts], rest[n_parts]

    @pl.when(pl.program_id(0) == 0)
    def _():
        out_ref[...] = prev_ref[...]

    gate_act = jnp.concatenate([p[1] for p in parts], axis=0)
    up_act = jnp.concatenate([p[2] for p in parts], axis=0)
    out_ref[...] += dot_nt(gate_act, mask_rows(gate_ref[...], gk_ref[...], BLK)) + dot_nt(
        up_act, mask_rows(up_ref[...], uk_ref[...], BLK)
    )


def grad_tokens_of(prev, gate_w, up_w, gk, uk, parts, starts, first, tiles, tile):
    rows, feats = prev.shape
    span = tiles * tile
    return pl.pallas_call(
        functools.partial(grad_tokens_kernel, len(parts)),
        out_shape=jax.ShapeDtypeStruct((rows, feats), F32),
        grid=(tiles,),
        in_specs=[
            pl.BlockSpec((rows, feats), lambda i: (0, 0)),
            pl.BlockSpec((feats, tile), lambda i: (0, first + i)),
            pl.BlockSpec((feats, tile), lambda i: (0, first + i)),
            pl.BlockSpec((gk.shape[0], tile), lambda i: (0, first + i)),
            pl.BlockSpec((uk.shape[0], tile), lambda i: (0, first + i)),
        ]
        + [
            pl.BlockSpec((3, p.shape[1], tile), functools.partial(lambda s, i: (0, 0, first - s + i), s))
            for p, s in zip(parts, starts)
        ],
        out_specs=pl.BlockSpec((rows, feats), lambda i: (0, 0)),
        compiler_params=params(),
        cost_estimate=pl.CostEstimate(
            flops=4 * rows * feats * span, bytes_accessed=4 * feats * span + 8 * rows * feats, transcendentals=0
        ),
        name="grad_tokens",
    )(prev, gate_w, up_w, gk, uk, *parts)


def weight_grads_kernel(n_parts, n_prev, xt_ref, og_ref, gk_ref, uk_ref, dk_ref, *rest):
    parts = rest[:n_parts]
    gate_ref, up_ref, down_ref = rest[n_parts + n_prev :]
    granule = down_ref.shape[0] // dk_ref.shape[1]
    xt = xt_ref[...]
    hidden = jnp.concatenate([p[0] for p in parts], axis=0)
    gate_act = jnp.concatenate([p[1] for p in parts], axis=0)
    up_act = jnp.concatenate([p[2] for p in parts], axis=0)
    gate_ref[...] = mask_rows(
        jnp.dot(xt, gate_act, preferred_element_type=F32).astype(BF), gk_ref[...], BLK
    )
    up_ref[...] = mask_rows(jnp.dot(xt, up_act, preferred_element_type=F32).astype(BF), uk_ref[...], BLK)
    down_ref[...] = mask_rows(dot_tn(hidden, og_ref[...]).astype(BF), dk_ref[0], granule)


def weight_grads(prev, xt, og, gk, uk, dk, parts, starts, first, tiles, tile, units):
    feats, rows = xt.shape
    span = tiles * tile
    n_prev = 0 if prev is None else 3
    base = 5 + len(parts)
    return pl.pallas_call(
        functools.partial(weight_grads_kernel, len(parts), n_prev),
        out_shape=(
            jax.ShapeDtypeStruct((feats, units), BF),
            jax.ShapeDtypeStruct((feats, units), BF),
            jax.ShapeDtypeStruct((units, feats), BF),
        ),
        grid=(tiles,),
        in_specs=[
            pl.BlockSpec((feats, rows), lambda i: (0, 0)),
            pl.BlockSpec((rows, feats), lambda i: (0, 0)),
            pl.BlockSpec((gk.shape[0], tile), lambda i: (0, first + i)),
            pl.BlockSpec((uk.shape[0], tile), lambda i: (0, first + i)),
            pl.BlockSpec((1,) + dk.shape[1:], lambda i: (first + i, 0, 0)),
        ]
        + [
            pl.BlockSpec((3, p.shape[1], tile), functools.partial(lambda s, i: (0, 0, first - s + i), s))
            for p, s in zip(parts, starts)
        ]
        + [pl.BlockSpec(memory_space=pl.ANY)] * n_prev,
        out_specs=[
            pl.BlockSpec((feats, tile), lambda i: (0, first + i)),
            pl.BlockSpec((feats, tile), lambda i: (0, first + i)),
            pl.BlockSpec((tile, feats), lambda i: (first + i, 0)),
        ],
        input_output_aliases={base + k: k for k in range(n_prev)},
        compiler_params=params(),
        cost_estimate=pl.CostEstimate(
            flops=6 * rows * feats * span, bytes_accessed=6 * feats * span + 4 * rows * feats, transcendentals=0
        ),
        name="weight_grads",
    )(xt, og, gk, uk, dk, *parts, *(() if prev is None else prev))


def pointwise(total):
    gate_pre, up_pre, hidden_grad = total[0], total[1], total[2]
    sigmoid_gate = jax.nn.sigmoid(gate_pre)
    active = gate_pre * sigmoid_gate
    hidden = (active * up_pre).astype(BF)
    grad_gate_act = (
        hidden_grad * up_pre * sigmoid_gate * (1.0 + gate_pre * (1.0 - sigmoid_gate))
    ).astype(BF)
    grad_up_act = (hidden_grad * active).astype(BF)
    return jnp.stack([hidden, grad_gate_act, grad_up_act])


def chunks_of(tiles, sizes):
    out, first = [], 0
    for size in sizes:
        size = min(size, tiles - first)
        if size > 0:
            out.append((first, size))
            first += size
    if first < tiles:
        out.append((first, tiles - first))
    return out


def local(n_row, n_col, tokens, out_grad, gate_w, up_w, down_w, gate_mask, up_mask, down_mask):
    rank_row, rank_col = lax.axis_index("row"), lax.axis_index("col")
    own, feats = tokens.shape
    units = gate_w.shape[1]
    half = own // 2
    n_chip = n_col // 2
    second_core = rank_col % 2 == 1
    tile = TILE if units % TILE == 0 else units
    tiles = units // tile
    granule = gcd_of(units, BLK)
    core_swap = [(i, i ^ 1) for i in range(n_col)]

    def swap_cores(value):
        return lax.ppermute(value, "col", core_swap)

    def swap_chips(value):
        total = value.astype(F32)
        for d in range(1, n_chip):
            other = lax.ppermute(value, "col", [(i, (i + 2 * d) % n_col) for i in range(n_col)])
            total = total + other.astype(F32)
        return total

    def mine_first(value):
        blocks = value.reshape(-1, 2, half, value.shape[1])
        first = jnp.where(second_core, blocks[:, 1], blocks[:, 0])
        last = jnp.where(second_core, blocks[:, 0], blocks[:, 1])
        return jnp.concatenate([first, last], axis=0).reshape(value.shape)

    def shifted(value, d):
        return lax.ppermute(value, "row", [(i, (i + d) % n_row) for i in range(n_row)])

    def gather_others(value):
        if n_row <= 8:
            return jnp.concatenate([shifted(value, d) for d in range(1, n_row)], axis=0)
        whole = lax.all_gather(value, "row", axis=0, tiled=True)
        others = [lax.rem(rank_row - d + n_row, n_row) for d in range(1, n_row)]
        return jnp.concatenate([lax.dynamic_slice_in_dim(whole, o * own, own, 0) for o in others], axis=0)

    col_first, row_first = rank_col * feats, rank_row * units
    feat_index = block_index(col_first, feats // BLK, BLK)
    lane_index = block_index(col_first, feats, 1)
    unit_lanes = block_index(row_first, units, 1)
    unit_index = block_index(row_first, units // granule, granule)
    gk = pick(gate_mask, feat_index, unit_lanes)
    uk = pick(up_mask, feat_index, unit_lanes)
    dk = pick(down_mask, unit_index, lane_index).reshape(tiles, tile // granule, feats)

    weights = (gate_w, up_w, down_w, gk, uk, dk)

    def exchange(x, og, first, size):
        keep, send = forward(x, og, *weights, first, size, tile)
        chip_sum = (keep.astype(F32) + swap_cores(send).astype(F32)).astype(BF)
        mine = pointwise(swap_chips(chip_sum))
        return mine, swap_cores(mine)

    x_own, og_own = mine_first(tokens), mine_first(out_grad)
    x_far, og_far = mine_first(gather_others(tokens)), mine_first(gather_others(out_grad))

    own_chunks = chunks_of(tiles, (2, 5))
    far_chunks = chunks_of(tiles, (2, 2, 2, 1))
    own_parts = [exchange(x_own, og_own, first, size) for first, size in own_chunks]
    far_parts = [exchange(x_far, og_far, first, size) for first, size in far_chunks]

    x_all = jnp.concatenate([x_own, x_far], axis=0)
    og_all = jnp.concatenate([og_own, og_far], axis=0)
    xt_all = x_all.T
    grads = None
    gt = jnp.zeros((x_all.shape[0], feats), F32)
    for own_first, own_size in own_chunks:
        pass

    def parts_at(first):
        for (f, s), pair in zip(own_chunks, own_parts):
            if f <= first < f + s:
                own_pair, own_start = pair, f
        for (f, s), pair in zip(far_chunks, far_parts):
            if f <= first < f + s:
                far_pair, far_start = pair, f
        return (*own_pair, *far_pair), (own_start, own_start, far_start, far_start)

    bounds = sorted({f for f, _ in own_chunks} | {f for f, _ in far_chunks} | {tiles})
    for first, last in zip(bounds[:-1], bounds[1:]):
        parts, starts = parts_at(first)
        gt = grad_tokens_of(gt, gate_w, up_w, gk, uk, parts, starts, first, last - first, tile)
        grads = weight_grads(grads, xt_all, og_all, gk, uk, dk, parts, starts, first, last - first, tile, units)

    gt = gt.astype(BF)
    far = gt[own:].reshape(2, n_row - 1, half, feats)
    total = gt[:own].astype(F32)
    if n_row <= 8:
        for d in range(1, n_row):
            piece = far[:, d - 1].reshape(own, feats)
            total = total + lax.ppermute(piece, "row", [(i, (i - d) % n_row) for i in range(n_row)]).astype(F32)
        total = total.astype(BF)
    else:
        order = jnp.concatenate([gt[:own].reshape(2, 1, half, feats), far], axis=1)
        order = jnp.swapaxes(order, 0, 1).reshape(n_row, own, feats)
        wanted = [lax.rem(rank_row - b + n_row, n_row) for b in range(n_row)]
        by_row = jnp.concatenate([lax.dynamic_slice_in_dim(order, w, 1, 0) for w in wanted], axis=0)
        total = lax.psum_scatter(by_row.reshape(n_row * own, feats), "row", scatter_dimension=0, tiled=True)
    total = mine_first(total)
    return (total, *grads)


def solution(mesh):
    in_specs = (
        P(("groups", "row"), "col"),
        P(("groups", "row"), "col"),
        P(("groups", "col"), "row"),
        P(("groups", "col"), "row"),
        P(("groups", "row"), "col"),
        P("groups", None),
        P("groups", None),
        P("groups", None),
    )
    out_specs = (
        P(("groups", "row"), "col"),
        P(("groups", "col"), "row"),
        P(("groups", "col"), "row"),
        P(("groups", "row"), "col"),
    )
    step = functools.partial(local, mesh.shape["row"], mesh.shape["col"])
    return jax.shard_map(step, mesh=mesh, in_specs=in_specs, out_specs=out_specs, check_vma=False)
```

```python
import functools

import jax
import jax.numpy as jnp
from jax import lax
from jax.experimental import pallas as pl
from jax.experimental.pallas import tpu as pltpu
from jax.sharding import PartitionSpec as P

BLK = 128
TILE = 512
COST_SCALE = 1000000000
OWN_CHUNKS = (7,)
FAR_CHUNKS = (2, 2, 2, 1)
BF = jnp.bfloat16
F32 = jnp.float32
ANY = pl.BlockSpec(memory_space=pl.ANY)
VMEM = pl.BlockSpec(memory_space=pltpu.VMEM)
SMEM = pl.BlockSpec(memory_space=pltpu.SMEM)


def params(mib=8):
    return pltpu.CompilerParams(vmem_limit_bytes=mib * 1024 * 1024)


def cost(flops, nbytes):
    return pl.CostEstimate(flops=int(flops) // COST_SCALE, bytes_accessed=int(nbytes) // COST_SCALE, transcendentals=0)


def gcd_of(a, b):
    while b:
        a, b = b, a % b
    return a


def in_vmem(value):
    return pltpu.with_memory_space_constraint(value, pltpu.VMEM)


def in_hbm(value):
    return pltpu.with_memory_space_constraint(value, pltpu.HBM)


def mask_rows(weight, keep, rows):
    return jnp.concatenate(
        [weight[i * rows : (i + 1) * rows, :] * keep[i : i + 1, :] for i in range(keep.shape[0])], axis=0
    )


def dot_nt(left, right):
    return lax.dot_general(left, right, (((1,), (1,)), ((), ())), preferred_element_type=F32)


def dot_tn(left, right):
    return lax.dot_general(left, right, (((0,), (0,)), ((), ())), preferred_element_type=F32)


def both_halves(blocks, half, second):
    low = [b[:half] for b in blocks]
    high = [b[half:] for b in blocks]
    mine = [jnp.where(second, h, l) for l, h in zip(low, high)]
    theirs = [jnp.where(second, l, h) for l, h in zip(low, high)]
    return jnp.concatenate(mine + theirs, axis=0)


def far_blocks(refs, k, own):
    return [r[k, b * own : (b + 1) * own, :] for r in refs for b in range(r.shape[1] // own)]


def one_hot(shape, match):
    return jnp.where(match, jnp.ones(shape, F32), jnp.zeros(shape, F32)).astype(BF)


def live(mask_ref):
    return jnp.where(mask_ref[...] > 0, 1.0, 0.0).astype(BF)


def open_kernel(n_deps, first, tiles, tile, place, x_ref, og_ref, gate_ref, up_ref, down_ref, gm_ref, um_ref, dm_ref, *rest):
    keep_ref, *send_refs, wg_ref, wu_ref, wd_ref, gk_ref, uk_ref, dk_ref, tok_ref, sems = rest[n_deps:]
    half = keep_ref.shape[1]
    feats = x_ref.shape[1]
    blocks = feats // BLK
    granules = dk_ref.shape[1]
    granule = tile // granules
    span = tiles * tile
    feat_block, unit_first, second = place[0], place[1] + first * tile, place[2] > 0

    def copies(t):
        if tiles == 1:
            here, there = pl.ds(first * tile, tile), pl.ds(0, tile)
        else:
            here = pl.ds(pl.multiple_of((first + t) * tile, tile), tile)
            there = pl.ds(pl.multiple_of(t * tile, tile), tile)
        return (
            pltpu.make_async_copy(gate_ref.at[:, here], wg_ref.at[:, there], sems.at[0, t]),
            pltpu.make_async_copy(up_ref.at[:, here], wu_ref.at[:, there], sems.at[1, t]),
            pltpu.make_async_copy(down_ref.at[here, :], wd_ref.at[there, :], sems.at[2, t]),
        )

    for t in range(tiles):
        for copy in copies(t):
            copy.start()

    tok_ref[...] = jnp.zeros_like(tok_ref)
    n_feat, n_unit = gm_ref.shape
    iota = lax.broadcasted_iota
    rows = one_hot((blocks, n_feat), iota(jnp.int32, (blocks, n_feat), 1) == feat_block + iota(jnp.int32, (blocks, n_feat), 0))
    lanes = one_hot((n_unit, span), iota(jnp.int32, (n_unit, span), 0) == (unit_first + iota(jnp.int32, (n_unit, span), 1)) // BLK)
    for m_ref, r_ref in ((gm_ref, gk_ref), (um_ref, uk_ref)):
        picked = jnp.dot(rows, live(m_ref), preferred_element_type=F32).astype(BF)
        r_ref[...] = jnp.dot(picked, lanes, preferred_element_type=F32).astype(BF)
    count = tiles * granules
    rows = one_hot((count, n_unit), iota(jnp.int32, (count, n_unit), 1) == (unit_first + iota(jnp.int32, (count, n_unit), 0) * granule) // BLK)
    lanes = one_hot((n_feat, feats), iota(jnp.int32, (n_feat, feats), 0) == feat_block + iota(jnp.int32, (n_feat, feats), 1) // BLK)
    picked = dot_nt(rows, live(dm_ref)).astype(BF)
    down_keep = jnp.dot(picked, lanes, preferred_element_type=F32).astype(BF)
    for t in range(tiles):
        dk_ref[t] = down_keep[t * granules : (t + 1) * granules]

    x = both_halves([x_ref[...]], half, second)
    og = both_halves([og_ref[...]], half, second)

    for t in range(tiles):
        here = pl.ds(t * tile, tile)
        arrivals = copies(t)
        for k, (w_ref, r_ref) in enumerate(((wg_ref, gk_ref), (wu_ref, uk_ref))):
            arrivals[k].wait()
            weight = mask_rows(w_ref[:, here], r_ref[:, here], BLK)
            w_ref[:, here] = weight
            part = jnp.dot(x, weight, preferred_element_type=F32).astype(BF)
            keep_ref[k, :, here] = part[:half]
            send_refs[k][:, here] = part[half:]
        arrivals[2].wait()
        weight = mask_rows(wd_ref[here, :], dk_ref[t], granule)
        wd_ref[here, :] = weight
        part = dot_nt(og, weight).astype(BF)
        keep_ref[2, :, here] = part[:half]
        send_refs[2][:, here] = part[half:]


TOKEN = jax.ShapeDtypeStruct((8, 128), F32)


def open_weights(place, x, og, gate_w, up_w, down_w, gm, um, dm, first, tiles, tile, granule, deps):
    rows, feats = x.shape
    half = rows // 2
    span = tiles * tile
    out = jax.ShapeDtypeStruct((3, half, span), BF)
    send = jax.ShapeDtypeStruct((half, span), BF)
    return pl.pallas_call(
        functools.partial(open_kernel, len(deps), first, tiles, tile),
        out_shape=(
            out,
            send,
            send,
            send,
            pltpu.VMEM((feats, span), BF),
            pltpu.VMEM((feats, span), BF),
            pltpu.VMEM((span, feats), BF),
            jax.ShapeDtypeStruct((feats // BLK, span), BF),
            jax.ShapeDtypeStruct((feats // BLK, span), BF),
            jax.ShapeDtypeStruct((tiles, tile // granule, feats), BF),
            TOKEN,
        ),
        in_specs=[SMEM, VMEM, VMEM, ANY, ANY, ANY, VMEM, VMEM, VMEM] + [ANY] * len(deps),
        out_specs=[VMEM] * 11,
        scratch_shapes=[pltpu.SemaphoreType.DMA((3, tiles))],
        compiler_params=params(),
        cost_estimate=cost(6 * rows * feats * span, 6 * feats * span),
        name="open_weights",
    )(place, x, og, in_hbm(gate_w), in_hbm(up_w), in_hbm(down_w), gm, um, dm, *deps)


def forward_kernel(n_far, own, offset, span, place, wg_ref, wu_ref, wd_ref, *rest):
    refs = rest[:n_far]
    keep_ref, *send_refs, tok_ref = rest[-5:]
    half = keep_ref.shape[1]
    second = place[2] > 0
    tok_ref[...] = jnp.zeros_like(tok_ref)
    x = both_halves(far_blocks(refs, 0, own), own // 2, second)
    here = pl.ds(offset, span)

    def put(k, value):
        value = value.astype(BF)
        keep_ref[k] = value[:half]
        send_refs[k][...] = value[half:]

    put(0, jnp.dot(x, wg_ref[:, here], preferred_element_type=F32))
    put(1, jnp.dot(x, wu_ref[:, here], preferred_element_type=F32))
    og = both_halves(far_blocks(refs, 1, own), own // 2, second)
    put(2, dot_nt(og, wd_ref[here, :]))


def forward(place, far, own, wg, wu, wd, offset, span, deps):
    rows, feats = sum(f.shape[1] for f in far), wg.shape[0]
    out = jax.ShapeDtypeStruct((3, rows // 2, span), BF)
    send = jax.ShapeDtypeStruct((rows // 2, span), BF)
    return pl.pallas_call(
        functools.partial(forward_kernel, len(far), own, offset, span),
        out_shape=(out, send, send, send, TOKEN),
        in_specs=[SMEM] + [VMEM] * (3 + len(far)) + [ANY] * len(deps),
        out_specs=[VMEM] * 5,
        compiler_params=params(),
        cost_estimate=cost(6 * rows * feats * span, 6 * feats * span),
        name="forward",
    )(place, in_vmem(wg), in_vmem(wu), in_vmem(wd), *far, *deps)


def tokens_kernel(n_far, own, place, x_ref, og_ref, *rest):
    refs = rest[:n_far]
    xt_ref, all_ref, tok_ref = rest[-3:]
    second = place[2] > 0
    tok_ref[...] = jnp.zeros_like(tok_ref)
    half = own // 2
    for k, mine in ((0, x_ref), (1, og_ref)):
        whole = jnp.concatenate(
            [both_halves([mine[...]], half, second), both_halves(far_blocks(refs, k, own), half, second)], axis=0
        )
        if k == 0:
            xt_ref[...] = whole.T
        else:
            all_ref[...] = whole


def all_tokens(place, x, og, far, deps):
    own, feats = x.shape
    rows = own + sum(f.shape[1] for f in far)
    return pl.pallas_call(
        functools.partial(tokens_kernel, len(far), own),
        out_shape=(jax.ShapeDtypeStruct((feats, rows), BF), jax.ShapeDtypeStruct((rows, feats), BF), TOKEN),
        in_specs=[SMEM] + [VMEM] * (2 + len(far)) + [ANY] * len(deps),
        out_specs=[VMEM] * 3,
        compiler_params=params(),
        cost_estimate=cost(rows * feats, 8 * rows * feats),
        name="all_tokens",
    )(place, x, og, *far, *deps)


def sum_kernel(keep_ref, *rest):
    others, out_ref = rest[:3], rest[3]
    for k, other in enumerate(others):
        out_ref[k] = (keep_ref[k].astype(F32) + other[...].astype(F32)).astype(BF)


def sum_of(keep, others):
    return pl.pallas_call(
        sum_kernel,
        out_shape=jax.ShapeDtypeStruct(keep.shape, BF),
        in_specs=[VMEM] * 4,
        out_specs=VMEM,
        compiler_params=params(),
        cost_estimate=cost(keep.size, 6 * keep.size),
        name="sum_cores",
    )(keep, *others)


def pointwise_kernel(n_other, sum_ref, *rest):
    others, (hidden_ref, gate_ref, up_ref, tok_ref) = rest[:n_other], rest[-4:]
    rows = hidden_ref.shape[0]
    tok_ref[...] = jnp.zeros_like(tok_ref)

    def step(here):
        total = [sum_ref[k, here, :].astype(F32) for k in range(3)]
        for other in others:
            total = [total[k] + other[k, here, :].astype(F32) for k in range(3)]
        gate_pre, up_pre, hidden_grad = total
        sigmoid_gate = jax.nn.sigmoid(gate_pre)
        active = gate_pre * sigmoid_gate
        hidden_ref[here, :] = (active * up_pre).astype(BF)
        gate_ref[here, :] = (
            hidden_grad * up_pre * sigmoid_gate * (1.0 + gate_pre * (1.0 - sigmoid_gate))
        ).astype(BF)
        up_ref[here, :] = (hidden_grad * active).astype(BF)

    if rows == 16:
        step(pl.ds(0, rows))
    else:

        @pl.loop(0, rows // 16)
        def _(i):
            step(pl.ds(pl.multiple_of(i * 16, 16), 16))


def pointwise(chip_sum, others, deps):
    return pl.pallas_call(
        functools.partial(pointwise_kernel, len(others)),
        out_shape=(*[jax.ShapeDtypeStruct(chip_sum.shape[1:], BF)] * 3, TOKEN),
        in_specs=[VMEM] * (1 + len(others)) + [ANY] * len(deps),
        out_specs=[VMEM] * 4,
        compiler_params=params(),
        cost_estimate=cost(20 * chip_sum.size, 6 * chip_sum.size),
        name="pointwise",
    )(chip_sum, *others, *deps)


def grad_tokens_kernel(offsets, weight_offset, span, prev_ref, wg_ref, wu_ref, *rest):
    n = len(offsets)
    gates, ups, (out_ref, tok_ref) = rest[:n], rest[n : 2 * n], rest[-2:]
    tok_ref[...] = jnp.zeros_like(tok_ref)
    here = pl.ds(weight_offset, span)
    gate_act = jnp.concatenate([p[:, s : s + span] for p, s in zip(gates, offsets)], axis=0)
    up_act = jnp.concatenate([p[:, s : s + span] for p, s in zip(ups, offsets)], axis=0)
    add = dot_nt(gate_act, wg_ref[:, here]) + dot_nt(up_act, wu_ref[:, here])
    if prev_ref is None:
        out_ref[...] = add
    else:
        out_ref[...] = prev_ref[...] + add


def grad_tokens_of(prev, wg, wu, weight_offset, parts, offsets, span, deps):
    rows = sum(p[1].shape[0] for p in parts)
    feats = wg.shape[0]
    kernel = functools.partial(grad_tokens_kernel, offsets, weight_offset, span)
    prevs = (prev,)
    if prev is None:
        kernel, prevs = functools.partial(kernel, None), ()
    return pl.pallas_call(
        kernel,
        out_shape=(jax.ShapeDtypeStruct((rows, feats), F32), TOKEN),
        in_specs=[VMEM] * (len(prevs) + 2 + 2 * len(parts)) + [ANY] * len(deps),
        out_specs=[VMEM] * 2,
        compiler_params=params(),
        cost_estimate=cost(4 * rows * feats * span, 4 * feats * span),
        name="grad_tokens",
    )(*prevs, in_vmem(wg), in_vmem(wu), *[p[1] for p in parts], *[p[2] for p in parts], *deps)


def weight_grads_kernel(n_parts, xt_ref, og_ref, gk_ref, uk_ref, dk_ref, *rest):
    n = n_parts
    hidden, gate_act, up_act = [
        jnp.concatenate([p[...] for p in rest[k * n : (k + 1) * n]], axis=0) for k in range(3)
    ]
    gate_ref, up_ref, down_ref, tok_ref = rest[-4:]
    tok_ref[...] = jnp.zeros_like(tok_ref)
    granule = down_ref.shape[0] // dk_ref.shape[1]
    xt = xt_ref[...]
    gate_ref[...] = mask_rows(
        jnp.dot(xt, gate_act, preferred_element_type=F32).astype(BF), gk_ref[...], BLK
    )
    up_ref[...] = mask_rows(jnp.dot(xt, up_act, preferred_element_type=F32).astype(BF), uk_ref[...], BLK)
    down_ref[...] = mask_rows(dot_tn(hidden, og_ref[...]).astype(BF), dk_ref[0], granule)


def weight_grads(prev, xt, og, gk, uk, dk, weight_start, parts, starts, first, tiles, tile, units, deps):
    feats, rows = xt.shape
    span = tiles * tile
    n_prev = 0 if prev is None else 3
    base = 5 + 3 * len(parts)

    def moved(s, i):
        return (0, s + i)

    return pl.pallas_call(
        functools.partial(weight_grads_kernel, len(parts)),
        out_shape=(
            pltpu.HBM((feats, units), BF),
            pltpu.HBM((feats, units), BF),
            pltpu.HBM((units, feats), BF),
            TOKEN,
        ),
        grid=(tiles,),
        in_specs=[
            pl.BlockSpec((feats, rows), lambda i: (0, 0)),
            pl.BlockSpec((rows, feats), lambda i: (0, 0)),
            pl.BlockSpec((gk.shape[0], tile), lambda i: (0, weight_start + i)),
            pl.BlockSpec((uk.shape[0], tile), lambda i: (0, weight_start + i)),
            pl.BlockSpec((1,) + dk.shape[1:], lambda i: (weight_start + i, 0, 0)),
        ]
        + [pl.BlockSpec((p[0].shape[0], tile), functools.partial(moved, s)) for p, s in zip(parts, starts)] * 3
        + [ANY] * (n_prev + len(deps)),
        out_specs=[
            pl.BlockSpec((feats, tile), lambda i: (0, first + i)),
            pl.BlockSpec((feats, tile), lambda i: (0, first + i)),
            pl.BlockSpec((tile, feats), lambda i: (first + i, 0)),
            pl.BlockSpec((8, 128), lambda i: (0, 0)),
        ],
        input_output_aliases={base + k: k for k in range(n_prev)},
        compiler_params=params(16),
        cost_estimate=cost(6 * rows * feats * span, 6 * feats * span),
        name="weight_grads",
    )(xt, og, gk, uk, dk, *[p[k] for k in range(3) for p in parts], *(() if prev is None else map(in_hbm, prev)), *deps)


def chunks_of(tiles, sizes):
    out, first = [], 0
    for size in sizes:
        size = min(size, tiles - first)
        if size > 0:
            out.append((first, size))
            first += size
    if first < tiles:
        out.append((first, tiles - first))
    return out


def local(n_row, n_col, tokens, out_grad, gate_w, up_w, down_w, gate_mask, up_mask, down_mask):
    rank_row, rank_col = lax.axis_index("row"), lax.axis_index("col")
    own, feats = tokens.shape
    units = gate_w.shape[1]
    half = own // 2
    n_chip = n_col // 2
    second_core = rank_col % 2 == 1
    tile = TILE if units % TILE == 0 else units
    tiles = units // tile
    granule = gcd_of(units, BLK)
    core_swap = [(i, i ^ 1) for i in range(n_col)]

    def swap_cores(values):
        return [lax.ppermute(value, "col", core_swap) for value in values]

    def from_chips(value):
        return [
            lax.ppermute(value, "col", [(i, (i + 2 * d) % n_col) for i in range(n_col)])
            for d in range(1, n_chip)
        ]

    both = jnp.stack([tokens, out_grad])
    if n_row <= 8:
        far = [lax.ppermute(both, "row", [(i, (i + d) % n_row) for i in range(n_row)]) for d in range(1, n_row)]
    else:
        whole = lax.all_gather(both, "row", axis=1, tiled=True)
        wanted = [lax.rem(rank_row - d + n_row, n_row) for d in range(1, n_row)]
        far = [jnp.concatenate([lax.dynamic_slice_in_dim(whole, w * own, own, 1) for w in wanted], axis=1)]

    place = jnp.stack([rank_col * (feats // BLK), rank_row * units, rank_col % 2]).astype(jnp.int32)
    masks = (gate_mask, up_mask, down_mask.T)

    own_chunks = chunks_of(tiles, OWN_CHUNKS)
    far_chunks = chunks_of(tiles, FAR_CHUNKS)

    def group_of(first):
        for g, (f, s) in enumerate(own_chunks):
            if f <= first < f + s:
                return g, first - f

    groups, own_sums, own_others, deps = [], [], [], ()
    for first, size in own_chunks:
        keep, *send, tok = open_weights(
            place, tokens, out_grad, gate_w, up_w, down_w, *masks, first, size, tile, granule, deps
        )
        send, group = send[:3], send[3:]
        groups.append(group)
        own_sums.append(sum_of(keep, swap_cores(send)))
        own_others.append(from_chips(own_sums[-1]))
        deps = (own_sums[-1],)

    far_sums, far_others, waiting = [], [], None
    for first, size in far_chunks:
        g, offset = group_of(first)
        keep, *send, tok = forward(place, far, own, *groups[g][:3], offset * tile, size * tile, deps)
        deps = (tok,)
        if waiting is not None:
            far_sums.append(sum_of(*waiting))
            far_others.append(from_chips(far_sums[-1]))
            deps += (far_sums[-1],)
        waiting = (keep, swap_cores(send))
    far_sums.append(sum_of(*waiting))
    far_others.append(from_chips(far_sums[-1]))

    xt_all, og_all, tok = all_tokens(place, tokens, out_grad, far, deps)
    deps = (tok, far_sums[-1])
    own_parts = []
    for chip_sum, other in zip(own_sums, own_others):
        *mine, tok = pointwise(chip_sum, other, deps)
        own_parts.append((mine, swap_cores(mine)))
        deps = (tok,)

    grads, gt, pending = None, None, []

    def flush(grads, work, deps):
        first, size, g, offset, parts, starts = work
        *grads, tok = weight_grads(
            grads, xt_all, og_all, *groups[g][3:], offset, parts, starts, first, size, tile, units, deps
        )
        return grads, (tok,)

    for c, (first, size) in enumerate(far_chunks):
        g, offset = group_of(first)
        *mine, tok = pointwise(far_sums[c], far_others[c], deps)
        deps = (tok,)
        parts = (*own_parts[g], mine, swap_cores(mine))
        if pending and c < len(far_chunks) - 1:
            grads, deps = flush(grads, pending.pop(0), deps)
        gt, tok = grad_tokens_of(
            gt, *groups[g][:2], offset * tile, parts, (offset * tile, offset * tile, 0, 0), size * tile, deps
        )
        deps = (tok,)
        pending.append((first, size, g, offset, parts, (offset, offset, 0, 0)))
    for work in pending:
        grads, deps = flush(grads, work, deps)

    gt = gt.astype(BF)
    far = gt[own:].reshape(2, n_row - 1, half, feats)
    total = gt[:own].astype(F32)
    if n_row <= 8:
        for d in range(1, n_row):
            piece = far[:, d - 1].reshape(own, feats)
            total = total + lax.ppermute(piece, "row", [(i, (i - d) % n_row) for i in range(n_row)]).astype(F32)
        total = total.astype(BF)
    else:
        order = jnp.concatenate([gt[:own].reshape(2, 1, half, feats), far], axis=1)
        order = jnp.swapaxes(order, 0, 1).reshape(n_row, own, feats)
        wanted = [lax.rem(rank_row - b + n_row, n_row) for b in range(n_row)]
        by_row = jnp.concatenate([lax.dynamic_slice_in_dim(order, w, 1, 0) for w in wanted], axis=0)
        total = lax.psum_scatter(by_row.reshape(n_row * own, feats), "row", scatter_dimension=0, tiled=True)
    low, high = total[:half], total[half:]
    total = jnp.concatenate([jnp.where(second_core, high, low), jnp.where(second_core, low, high)], axis=0)
    return (total, *grads)


def solution(mesh):
    in_specs = (
        P(("groups", "row"), "col"),
        P(("groups", "row"), "col"),
        P(("groups", "col"), "row"),
        P(("groups", "col"), "row"),
        P(("groups", "row"), "col"),
        P("groups", None),
        P("groups", None),
        P("groups", None),
    )
    out_specs = (
        P(("groups", "row"), "col"),
        P(("groups", "col"), "row"),
        P(("groups", "col"), "row"),
        P(("groups", "row"), "col"),
    )
    step = functools.partial(local, mesh.shape["row"], mesh.shape["col"])
    return jax.shard_map(step, mesh=mesh, in_specs=in_specs, out_specs=out_specs, check_vma=False)
```

```python
import functools

import jax
import jax.numpy as jnp
from jax import lax
from jax.experimental import pallas as pl
from jax.experimental.pallas import tpu as pltpu
from jax.sharding import PartitionSpec as P

BLK = 128
TILE = 512
LANE = 16
AHEAD = 2
COST_SCALE = 1000000000
OWN_CHUNKS = (4, 3)
OWN_PIECES = (((0,), (1,), (2,)), ((0, 1), (2,)))
OWN_AFTER = (0, 2)
FAR_PIECES = ((0,), (1,), (2,))
FAR_CHUNKS = (2, 2, 2, 1)
BF = jnp.bfloat16
F32 = jnp.float32
ANY = pl.BlockSpec(memory_space=pl.ANY)
VMEM = pl.BlockSpec(memory_space=pltpu.VMEM)
SMEM = pl.BlockSpec(memory_space=pltpu.SMEM)


def params(mib=8):
    return pltpu.CompilerParams(vmem_limit_bytes=mib * 1024 * 1024)


def cost(flops, nbytes):
    return pl.CostEstimate(flops=int(flops) // COST_SCALE, bytes_accessed=int(nbytes) // COST_SCALE, transcendentals=0)


def gcd_of(a, b):
    while b:
        a, b = b, a % b
    return a


def in_vmem(value):
    return pltpu.with_memory_space_constraint(value, pltpu.VMEM)


def in_hbm(value):
    return pltpu.with_memory_space_constraint(value, pltpu.HBM)


def mask_rows(weight, keep, rows):
    pieces = []
    for i in range(weight.shape[0] // rows):
        mask = keep[LANE * i : LANE * (i + 1), :]
        pieces += [weight[i * rows + g : i * rows + g + LANE, :] * mask for g in range(0, rows, LANE)]
    return jnp.concatenate(pieces, axis=0)


def dot_nt(left, right):
    return lax.dot_general(left, right, (((1,), (1,)), ((), ())), preferred_element_type=F32)


def dot_tn(left, right):
    return lax.dot_general(left, right, (((0,), (0,)), ((), ())), preferred_element_type=F32)


def both_halves(blocks, half, second):
    low = [b[:half] for b in blocks]
    high = [b[half:] for b in blocks]
    mine = [jnp.where(second, h, l) for l, h in zip(low, high)]
    theirs = [jnp.where(second, l, h) for l, h in zip(low, high)]
    return jnp.concatenate(mine + theirs, axis=0)


def far_blocks(refs, k, own):
    return [r[k, b * own : (b + 1) * own, :] for r in refs for b in range(r.shape[1] // own)]


def one_hot(shape, match):
    return jnp.where(match, jnp.ones(shape, F32), jnp.zeros(shape, F32)).astype(BF)


def live(mask_ref):
    return jnp.where(mask_ref[...] > 0, 1.0, 0.0).astype(BF)


def open_kernel(n_deps, pieces, opener, first, tiles, tile, granule, place, both_ref, gate_ref, up_ref, down_ref, *rest):
    keeps, rest = rest[:3], rest[3 + n_deps :]
    keep_ref, *sends = rest[: 1 + len(pieces)]
    rest = rest[1 + len(pieces) :]
    wg_ref, wu_ref, wd_ref, tok_ref = rest[:4]
    sems, rest = rest[-1], rest[4:-1]
    half, feats = keep_ref.shape[1], wg_ref.shape[0]
    granules = tile // granule

    def copies(t):
        here, there = pl.ds((first + t) * tile, tile), pl.ds(t * tile, tile)
        return (
            pltpu.make_async_copy(gate_ref.at[:, here], wg_ref.at[:, there], sems.at[0, t]),
            pltpu.make_async_copy(up_ref.at[:, here], wu_ref.at[:, there], sems.at[1, t]),
            pltpu.make_async_copy(down_ref.at[here, :], wd_ref.at[there, :], sems.at[2, t]),
        )

    if opener:
        gk_ref, uk_ref, dk_ref, gm_ref, um_ref, dm_ref, mask_sems = rest
        fetches = [pltpu.make_async_copy(a, b, mask_sems.at[i]) for i, (a, b) in enumerate(zip(keeps, (gm_ref, um_ref, dm_ref)))]
        for fetch in fetches:
            fetch.start()
    else:
        gk_ref, uk_ref, dk_ref = keeps
    for t in range(min(AHEAD, tiles)):
        for copy in copies(t):
            copy.start()
    tok_ref[...] = jnp.zeros_like(tok_ref)
    if opener:
        for fetch in fetches:
            fetch.wait()
        keep_rows(place, gm_ref, um_ref, dm_ref, gk_ref, uk_ref, dk_ref, granule)

    second = place[2] > 0
    x = both_halves([both_ref[0]], half, second)
    og = both_halves([both_ref[1]], half, second)

    def put(k, t, part):
        here = pl.ds(t * tile, tile)
        keep_ref[k, :, here] = part[:half]
        for ks, ref in zip(pieces, sends):
            if k in ks:
                ref[ks.index(k), :, here] = part[half:]

    for t in range(tiles):
        here, lanes = pl.ds(t * tile, tile), pl.ds((first + t) * tile, tile)
        arrivals = copies(t)
        for k, (w_ref, r_ref) in enumerate(((wg_ref, gk_ref), (wu_ref, uk_ref))):
            arrivals[k].wait()
            if t + AHEAD < tiles:
                copies(t + AHEAD)[k].start()
            weight = mask_rows(w_ref[:, here], r_ref[:, lanes], BLK)
            w_ref[:, here] = weight
            put(k, t, jnp.dot(x, weight, preferred_element_type=F32).astype(BF))
        arrivals[2].wait()
        if t + AHEAD < tiles:
            copies(t + AHEAD)[2].start()
        masks = pl.ds((first + t) * granules * LANE, granules * LANE)
        weight = mask_rows(wd_ref[here, :], dk_ref[masks, :], granule)
        wd_ref[here, :] = weight
        put(2, t, dot_nt(og, weight).astype(BF))


def keep_rows(place, gm_ref, um_ref, dm_ref, gk_ref, uk_ref, dk_ref, granule):
    feat_block, unit_first = place[0], place[1]
    n_feat, n_unit = gm_ref.shape
    units, feats = gk_ref.shape[1], dk_ref.shape[1]
    iota = lax.broadcasted_iota
    rows = (feats // BLK * LANE, n_feat)
    rows = one_hot(rows, iota(jnp.int32, rows, 1) == feat_block + iota(jnp.int32, rows, 0) // LANE)
    lanes = (n_unit, units)
    lanes = one_hot(lanes, iota(jnp.int32, lanes, 0) == (unit_first + iota(jnp.int32, lanes, 1)) // BLK)
    for m_ref, r_ref in ((gm_ref, gk_ref), (um_ref, uk_ref)):
        picked = jnp.dot(rows, live(m_ref), preferred_element_type=F32).astype(BF)
        r_ref[...] = jnp.dot(picked, lanes, preferred_element_type=F32).astype(BF)
    rows = (units // granule * LANE, n_unit)
    rows = one_hot(rows, iota(jnp.int32, rows, 1) == (unit_first + iota(jnp.int32, rows, 0) // LANE * granule) // BLK)
    lanes = (n_feat, feats)
    lanes = one_hot(lanes, iota(jnp.int32, lanes, 0) == feat_block + iota(jnp.int32, lanes, 1) // BLK)
    picked = dot_nt(rows, live(dm_ref)).astype(BF)
    dk_ref[...] = jnp.dot(picked, lanes, preferred_element_type=F32).astype(BF)


TOKEN = jax.ShapeDtypeStruct((8, 128), F32)


def open_weights(place, both, gate_w, up_w, down_w, masks, keeps, first, tiles, tile, granule, pieces, deps):
    _, rows, feats = both.shape
    units = gate_w.shape[1]
    half = rows // 2
    span = tiles * tile
    opener = keeps is None
    made = [
        jax.ShapeDtypeStruct((feats // BLK * LANE, units), BF),
        jax.ShapeDtypeStruct((feats // BLK * LANE, units), BF),
        jax.ShapeDtypeStruct((units // granule * LANE, feats), BF),
    ]
    scratch = [pltpu.VMEM(m.shape, m.dtype) for m in masks] + [pltpu.SemaphoreType.DMA((3,))]
    keep, *rest = pl.pallas_call(
        functools.partial(open_kernel, len(deps), pieces, opener, first, tiles, tile, granule),
        out_shape=(
            jax.ShapeDtypeStruct((3, half, span), BF),
            *[jax.ShapeDtypeStruct((len(ks), half, span), BF) for ks in pieces],
            pltpu.VMEM((feats, span), BF),
            pltpu.VMEM((feats, span), BF),
            pltpu.VMEM((span, feats), BF),
            TOKEN,
            *(made if opener else ()),
        ),
        in_specs=[SMEM, VMEM, ANY, ANY, ANY] + [ANY if opener else VMEM] * 3 + [ANY] * len(deps),
        out_specs=[VMEM] * (5 + len(pieces) + (3 if opener else 0)),
        scratch_shapes=(scratch if opener else []) + [pltpu.SemaphoreType.DMA((3, tiles))],
        compiler_params=params(),
        cost_estimate=cost(6 * rows * feats * span, 6 * feats * span),
        name="open_weights",
    )(place, both, *map(in_hbm, (gate_w, up_w, down_w)), *(map(in_hbm, masks) if opener else keeps), *deps)
    n = len(pieces)
    return keep, rest[:n], rest[n : n + 3], rest[n + 4 :] if opener else keeps


def forward_kernel(pieces, own, offset, span, x_ref, og_ref, wg_ref, wu_ref, wd_ref, *rest):
    keep_ref, *sends, tok_ref = rest[-2 - len(pieces) :]
    half = keep_ref.shape[1]
    tok_ref[...] = jnp.zeros_like(tok_ref)
    x = x_ref[own:, :]
    here = pl.ds(offset, span)

    def put(k, value):
        value = value.astype(BF)
        keep_ref[k] = value[:half]
        for ks, ref in zip(pieces, sends):
            if k in ks:
                ref[ks.index(k)] = value[half:]

    put(0, jnp.dot(x, wg_ref[:, here], preferred_element_type=F32))
    put(1, jnp.dot(x, wu_ref[:, here], preferred_element_type=F32))
    put(2, dot_nt(og_ref[own:, :], wd_ref[here, :]))


def forward(x_all, og_all, own, wg, wu, wd, offset, span, pieces, deps):
    rows, feats = x_all.shape[0] - own, x_all.shape[1]
    keep, *sends, tok = pl.pallas_call(
        functools.partial(forward_kernel, pieces, own, offset, span),
        out_shape=(
            jax.ShapeDtypeStruct((3, rows // 2, span), BF),
            *[jax.ShapeDtypeStruct((len(ks), rows // 2, span), BF) for ks in pieces],
            TOKEN,
        ),
        in_specs=[VMEM] * 5 + [ANY] * len(deps),
        out_specs=[VMEM] * (2 + len(pieces)),
        compiler_params=params(),
        cost_estimate=cost(6 * rows * feats * span, 6 * feats * span),
        name="forward",
    )(x_all, og_all, in_vmem(wg), in_vmem(wu), in_vmem(wd), *deps)
    return keep, sends, tok


def tokens_kernel(n_far, own, place, both_ref, *rest):
    refs = rest[:n_far]
    x_ref, xt_ref, og_ref, tok_ref = rest[-4:]
    second = place[2] > 0
    tok_ref[...] = jnp.zeros_like(tok_ref)
    half = own // 2
    for k, out_ref in ((0, x_ref), (1, og_ref)):
        whole = jnp.concatenate(
            [both_halves([both_ref[k]], half, second), both_halves(far_blocks(refs, k, own), half, second)], axis=0
        )
        out_ref[...] = whole
        if k == 0:
            xt_ref[...] = whole.T


def all_tokens(place, both, far, deps):
    _, own, feats = both.shape
    rows = own + sum(f.shape[1] for f in far)
    return pl.pallas_call(
        functools.partial(tokens_kernel, len(far), own),
        out_shape=(
            jax.ShapeDtypeStruct((rows, feats), BF),
            jax.ShapeDtypeStruct((feats, rows), BF),
            jax.ShapeDtypeStruct((rows, feats), BF),
            TOKEN,
        ),
        in_specs=[SMEM] + [VMEM] * (1 + len(far)) + [ANY] * len(deps),
        out_specs=[VMEM] * 4,
        compiler_params=params(),
        cost_estimate=cost(rows * feats, 8 * rows * feats),
        name="all_tokens",
    )(place, both, *far, *deps)


def sum_kernel(pieces, keep_ref, *rest):
    others, out_ref = rest[: len(pieces)], rest[-1]
    for ks, other in zip(pieces, others):
        for i, k in enumerate(ks):
            out_ref[k] = (keep_ref[k].astype(F32) + other[i].astype(F32)).astype(BF)


def sum_of(keep, others, pieces, deps):
    return pl.pallas_call(
        functools.partial(sum_kernel, pieces),
        out_shape=jax.ShapeDtypeStruct(keep.shape, BF),
        in_specs=[VMEM] * (1 + len(others)) + [ANY] * len(deps),
        out_specs=VMEM,
        compiler_params=params(),
        cost_estimate=cost(keep.size, 6 * keep.size),
        name="sum_cores",
    )(keep, *others, *deps)


def pointwise_kernel(n_other, sum_ref, *rest):
    others, (hidden_ref, gate_ref, up_ref, tok_ref) = rest[:n_other], rest[-4:]
    rows = hidden_ref.shape[0]
    tok_ref[...] = jnp.zeros_like(tok_ref)

    def step(here):
        total = [sum_ref[k, here, :].astype(F32) for k in range(3)]
        for other in others:
            total = [total[k] + other[k, here, :].astype(F32) for k in range(3)]
        gate_pre, up_pre, hidden_grad = total
        sigmoid_gate = jax.nn.sigmoid(gate_pre)
        active = gate_pre * sigmoid_gate
        hidden_ref[here, :] = (active * up_pre).astype(BF)
        gate_ref[here, :] = (
            hidden_grad * up_pre * sigmoid_gate * (1.0 + gate_pre * (1.0 - sigmoid_gate))
        ).astype(BF)
        up_ref[here, :] = (hidden_grad * active).astype(BF)

    if rows == 16:
        step(pl.ds(0, rows))
    else:

        @pl.loop(0, rows // 16)
        def _(i):
            step(pl.ds(pl.multiple_of(i * 16, 16), 16))


def pointwise(chip_sum, others, deps):
    return pl.pallas_call(
        functools.partial(pointwise_kernel, len(others)),
        out_shape=(*[jax.ShapeDtypeStruct(chip_sum.shape[1:], BF)] * 3, TOKEN),
        in_specs=[VMEM] * (1 + len(others)) + [ANY] * len(deps),
        out_specs=[VMEM] * 4,
        compiler_params=params(),
        cost_estimate=cost(20 * chip_sum.size, 6 * chip_sum.size),
        name="pointwise",
    )(chip_sum, *others, *deps)


def grad_tokens_kernel(offsets, weight_offset, span, own, n_out, prev_ref, wg_ref, wu_ref, *rest):
    n = len(offsets)
    gates, ups, (*outs, tok_ref) = rest[:n], rest[n : 2 * n], rest[-1 - n_out :]
    tok_ref[...] = jnp.zeros_like(tok_ref)
    here = pl.ds(weight_offset, span)
    gate_act = jnp.concatenate([p[:, s : s + span] for p, s in zip(gates, offsets)], axis=0)
    up_act = jnp.concatenate([p[:, s : s + span] for p, s in zip(ups, offsets)], axis=0)
    add = dot_nt(gate_act, wg_ref[:, here]) + dot_nt(up_act, wu_ref[:, here])
    if prev_ref is not None:
        add += prev_ref[...]
    if not own:
        outs[0][...] = add
        return
    half = own // 2
    blocks = outs[0].shape[0] // own
    outs[1][...] = add[:own]
    add = add.astype(BF)
    for b in range(blocks):
        for h in range(2):
            start = own + (h * blocks + b) * half
            outs[0][pl.ds(b * own + h * half, half), :] = add[start : start + half]


def grad_tokens_of(prev, wg, wu, weight_offset, parts, offsets, span, own, deps):
    rows = sum(p[1].shape[0] for p in parts)
    feats = wg.shape[0]
    outs = [jax.ShapeDtypeStruct((rows, feats), F32)]
    if own:
        outs = [jax.ShapeDtypeStruct((rows - own, feats), BF), jax.ShapeDtypeStruct((own, feats), F32)]
    kernel = functools.partial(grad_tokens_kernel, offsets, weight_offset, span, own, len(outs))
    prevs = (prev,)
    if prev is None:
        kernel, prevs = functools.partial(kernel, None), ()
    return pl.pallas_call(
        kernel,
        out_shape=(*outs, TOKEN),
        in_specs=[VMEM] * (len(prevs) + 2 + 2 * len(parts)) + [ANY] * len(deps),
        out_specs=[VMEM] * (1 + len(outs)),
        compiler_params=params(),
        cost_estimate=cost(4 * rows * feats * span, 4 * feats * span),
        name="grad_tokens",
    )(*prevs, in_vmem(wg), in_vmem(wu), *[p[1] for p in parts], *[p[2] for p in parts], *deps)


def weight_grads_kernel(n, granule, xt_ref, og_ref, gk_ref, uk_ref, dk_ref, *rest):
    gate_ref, up_ref, down_ref, tok_ref = rest[-4:]
    tok_ref[...] = jnp.zeros_like(tok_ref)
    hidden, gate_act, up_act = [
        jnp.concatenate([p[...] for p in rest[k * n : (k + 1) * n]], axis=0) for k in range(3)
    ]
    for act, keep, out_ref in ((gate_act, gk_ref, gate_ref), (up_act, uk_ref, up_ref)):
        value = jnp.dot(xt_ref[...], act, preferred_element_type=F32).astype(BF)
        out_ref[...] = mask_rows(value, keep[...], BLK)
    down_ref[...] = mask_rows(dot_tn(hidden, og_ref[...]).astype(BF), dk_ref[...], granule)


def weight_grads(prev, xt, og, gk, uk, dk, weight_start, parts, starts, first, tiles, tile, units, granule, deps):
    feats, rows = xt.shape
    span = tiles * tile
    n_prev = 0 if prev is None else 3
    base = 5 + 3 * len(parts)

    def moved(s, i):
        return (0, s + i)

    return pl.pallas_call(
        functools.partial(weight_grads_kernel, len(parts), granule),
        out_shape=(
            pltpu.HBM((feats, units), BF),
            pltpu.HBM((feats, units), BF),
            pltpu.HBM((units, feats), BF),
            TOKEN,
        ),
        grid=(tiles,),
        in_specs=[
            pl.BlockSpec((feats, rows), lambda i: (0, 0)),
            pl.BlockSpec((rows, feats), lambda i: (0, 0)),
            pl.BlockSpec((gk.shape[0], tile), lambda i: (0, weight_start + i)),
            pl.BlockSpec((uk.shape[0], tile), lambda i: (0, weight_start + i)),
            pl.BlockSpec((tile // granule * LANE, feats), lambda i: (weight_start + i, 0)),
        ]
        + [pl.BlockSpec((p[0].shape[0], tile), functools.partial(moved, s)) for p, s in zip(parts, starts)] * 3
        + [ANY] * (n_prev + len(deps)),
        out_specs=[
            pl.BlockSpec((feats, tile), lambda i: (0, first + i)),
            pl.BlockSpec((feats, tile), lambda i: (0, first + i)),
            pl.BlockSpec((tile, feats), lambda i: (first + i, 0)),
            pl.BlockSpec((8, 128), lambda i: (0, 0)),
        ],
        input_output_aliases={base + k: k for k in range(n_prev)},
        compiler_params=params(16),
        cost_estimate=cost(6 * rows * feats * span, 6 * feats * span),
        name="weight_grads",
    )(xt, og, gk, uk, dk, *[p[k] for k in range(3) for p in parts], *(() if prev is None else map(in_hbm, prev)), *deps)


def finish_kernel(place, own_ref, *rest):
    arrived, out_ref = rest[:-1], rest[-1]
    total = own_ref[...]
    for piece in arrived:
        total += piece[...].astype(F32)
    out_ref[...] = both_halves([total.astype(BF)], total.shape[0] // 2, place[2] > 0)


def finish(place, own, arrived):
    return pl.pallas_call(
        finish_kernel,
        out_shape=jax.ShapeDtypeStruct(own.shape, BF),
        in_specs=[SMEM] + [VMEM] * (1 + len(arrived)),
        out_specs=VMEM,
        compiler_params=params(),
        cost_estimate=cost(4 * own.size, 8 * own.size),
        name="finish",
    )(place, own, *arrived)


def chunks_of(tiles, sizes):
    out, first = [], 0
    for size in sizes:
        size = min(size, tiles - first)
        if size > 0:
            out.append((first, size))
            first += size
    if first < tiles:
        out.append((first, tiles - first))
    return out


def local(n_row, n_col, tokens, out_grad, gate_w, up_w, down_w, gate_mask, up_mask, down_mask):
    rank_row, rank_col = lax.axis_index("row"), lax.axis_index("col")
    own, feats = tokens.shape
    units = gate_w.shape[1]
    half = own // 2
    n_chip = n_col // 2
    tile = TILE if units % TILE == 0 else units
    tiles = units // tile
    granule = gcd_of(units, BLK)
    core_swap = [(i, i ^ 1) for i in range(n_col)]

    def swap_cores(values):
        return [lax.ppermute(value, "col", core_swap) for value in values]

    def flipped(value, d):
        return lax.ppermute(value, "row", [(i, i ^ d) for i in range(n_row)])

    def from_chips(value):
        return [
            lax.ppermute(value, "col", [(i, (i + 2 * d) % n_col) for i in range(n_col)])
            for d in range(1, n_chip)
        ]

    both = jnp.stack([tokens, out_grad])
    if n_row == 4:
        two = flipped(both, 2)
        far = [flipped(both, 1), two, flipped(two, 1)]
    else:
        whole = lax.all_gather(both, "row", axis=1, tiled=True)
        wanted = [rank_row ^ d for d in range(1, n_row)]
        far = [jnp.concatenate([lax.dynamic_slice_in_dim(whole, w * own, own, 1) for w in wanted], axis=1)]

    place = jnp.stack([rank_col * (feats // BLK), rank_row * units, rank_col % 2]).astype(jnp.int32)
    masks = (gate_mask, up_mask, down_mask.T)

    own_chunks = chunks_of(tiles, OWN_CHUNKS)
    far_chunks = chunks_of(tiles, FAR_CHUNKS)

    def group_of(first):
        for g, (f, s) in enumerate(own_chunks):
            if f <= first < f + s:
                return g, first - f

    groups, own_sums, own_others, keeps, deps = [], [], [], None, ()
    for c, (first, size) in enumerate(own_chunks):
        pieces = OWN_PIECES[min(c, len(OWN_PIECES) - 1)]
        keep, send, group, keeps = open_weights(
            place, both, gate_w, up_w, down_w, masks, keeps, first, size, tile, granule, pieces, deps
        )
        groups.append(group)
        own_sums.append(sum_of(keep, swap_cores(send), pieces, ()))
        own_others.append(from_chips(own_sums[-1]))
        deps = (own_sums[-1],)

    x_all, xt_all, og_all, tok = all_tokens(place, both, far, deps)
    deps = (tok,)
    far_sums, far_others, own_parts, waiting = [], [], [], None

    def open_own(c, deps):
        *mine, tok = pointwise(own_sums[c], own_others[c], deps)
        own_parts.append((mine, swap_cores(mine)))
        return (tok,)

    for first, size in far_chunks:
        g, offset = group_of(first)
        keep, send, tok = forward(x_all, og_all, own, *groups[g], offset * tile, size * tile, FAR_PIECES, deps)
        deps = (tok,)
        if waiting is not None:
            far_sums.append(sum_of(*waiting, FAR_PIECES, far_sums[-1:]))
            far_others.append(from_chips(far_sums[-1]))
            deps += (far_sums[-1],)
        waiting = (keep, swap_cores(send))
        if len(own_parts) < len(own_chunks) and len(far_sums) >= OWN_AFTER[len(own_parts)]:
            deps = open_own(len(own_parts), deps)
    far_sums.append(sum_of(*waiting, FAR_PIECES, far_sums[-1:]))
    far_others.append(from_chips(far_sums[-1]))

    deps = (far_sums[-1],)
    while len(own_parts) < len(own_chunks):
        deps = open_own(len(own_parts), deps)

    grads, gt, pending = None, None, []

    def flush(grads, work, deps):
        first, size, g, offset, parts, starts = work
        *grads, tok = weight_grads(
            grads, xt_all, og_all, *keeps, first, parts, starts, first, size, tile, units, granule, deps
        )
        return grads, (tok,)

    for c, (first, size) in enumerate(far_chunks):
        g, offset = group_of(first)
        *mine, tok = pointwise(far_sums[c], far_others[c], deps)
        deps = (tok,)
        parts = (*own_parts[g], mine, swap_cores(mine))
        last = c == len(far_chunks) - 1
        if pending:
            grads, deps = flush(grads, pending.pop(0), deps)
        offsets = (offset * tile, offset * tile, 0, 0)
        gt, *rest, tok = grad_tokens_of(
            gt, *groups[g][:2], offset * tile, parts, offsets, size * tile, own if last else 0, deps
        )
        deps = (tok,)
        pending.append((first, size, g, offset, parts, (offset, offset, 0, 0)))
    for work in pending:
        grads, deps = flush(grads, work, deps)

    if n_row == 4:
        arrived = [flipped(gt[(d - 1) * own : d * own], d) for d in range(1, n_row)]
    else:
        blocks = jnp.concatenate([rest[0].astype(BF), gt], axis=0).reshape(n_row, own, feats)
        wanted = [rank_row ^ b for b in range(n_row)]
        by_row = jnp.concatenate([lax.dynamic_slice_in_dim(blocks, w, 1, 0) for w in wanted], axis=0)
        arrived = [lax.psum_scatter(by_row.reshape(n_row * own, feats), "row", scatter_dimension=0, tiled=True)]
        rest = [jnp.zeros_like(rest[0])]
    return (finish(place, rest[0], arrived), *grads)


def solution(mesh):
    in_specs = (
        P(("groups", "row"), "col"),
        P(("groups", "row"), "col"),
        P(("groups", "col"), "row"),
        P(("groups", "col"), "row"),
        P(("groups", "row"), "col"),
        P("groups", None),
        P("groups", None),
        P("groups", None),
    )
    out_specs = (
        P(("groups", "row"), "col"),
        P(("groups", "col"), "row"),
        P(("groups", "col"), "row"),
        P(("groups", "row"), "col"),
    )
    step = functools.partial(local, mesh.shape["row"], mesh.shape["col"])
    return jax.shard_map(step, mesh=mesh, in_specs=in_specs, out_specs=out_specs, check_vma=False)
```

```python
import functools

import jax
import jax.numpy as jnp
from jax import lax
from jax.experimental import pallas as pl
from jax.experimental.pallas import tpu as pltpu
from jax.sharding import PartitionSpec as P

BLK = 128
TILE = 512
LANE = 16
AHEAD = 2
COST_SCALE = 1000000000
OWN_CHUNKS = (4, 3)
OWN_PIECES = (((0,), (1,), (2,)), ((0, 1), (2,)))
OWN_AFTER = (1, 2)
DEFER = True
FAR_PIECES = ((0,), (1,), (2,))
FAR_CHUNKS = (2, 2, 2, 1)
BF = jnp.bfloat16
F32 = jnp.float32
ANY = pl.BlockSpec(memory_space=pl.ANY)
VMEM = pl.BlockSpec(memory_space=pltpu.VMEM)
SMEM = pl.BlockSpec(memory_space=pltpu.SMEM)


def params(mib=8):
    return pltpu.CompilerParams(vmem_limit_bytes=mib * 1024 * 1024)


def cost(flops, nbytes):
    return pl.CostEstimate(flops=int(flops) // COST_SCALE, bytes_accessed=int(nbytes) // COST_SCALE, transcendentals=0)


def gcd_of(a, b):
    while b:
        a, b = b, a % b
    return a


def in_vmem(value):
    return pltpu.with_memory_space_constraint(value, pltpu.VMEM)


def in_hbm(value):
    return pltpu.with_memory_space_constraint(value, pltpu.HBM)


def mask_rows(weight, keep, rows):
    pieces = []
    for i in range(weight.shape[0] // rows):
        mask = keep[LANE * i : LANE * (i + 1), :]
        pieces += [weight[i * rows + g : i * rows + g + LANE, :] * mask for g in range(0, rows, LANE)]
    return jnp.concatenate(pieces, axis=0)


def dot_nt(left, right):
    return lax.dot_general(left, right, (((1,), (1,)), ((), ())), preferred_element_type=F32)


def dot_tn(left, right):
    return lax.dot_general(left, right, (((0,), (0,)), ((), ())), preferred_element_type=F32)


def both_halves(blocks, half, second):
    low = [b[:half] for b in blocks]
    high = [b[half:] for b in blocks]
    mine = [jnp.where(second, h, l) for l, h in zip(low, high)]
    theirs = [jnp.where(second, l, h) for l, h in zip(low, high)]
    return jnp.concatenate(mine + theirs, axis=0)


def far_blocks(refs, k, own):
    return [r[k, b * own : (b + 1) * own, :] for r in refs for b in range(r.shape[1] // own)]


def one_hot(shape, match):
    return jnp.where(match, jnp.ones(shape, F32), jnp.zeros(shape, F32)).astype(BF)


def live(mask_ref):
    return jnp.where(mask_ref[...] > 0, 1.0, 0.0).astype(BF)


def open_kernel(n_deps, pieces, opener, first, tiles, tile, granule, place, both_ref, gate_ref, up_ref, down_ref, *rest):
    keeps, rest = rest[:3], rest[3 + n_deps :]
    keep_ref, *sends = rest[: 1 + len(pieces)]
    rest = rest[1 + len(pieces) :]
    wg_ref, wu_ref, wd_ref, tok_ref = rest[:4]
    sems, rest = rest[-1], rest[4:-1]
    half, feats = keep_ref.shape[1], wg_ref.shape[0]
    granules = tile // granule

    def copies(t):
        here, there = pl.ds((first + t) * tile, tile), pl.ds(t * tile, tile)
        return (
            pltpu.make_async_copy(gate_ref.at[:, here], wg_ref.at[:, there], sems.at[0, t]),
            pltpu.make_async_copy(up_ref.at[:, here], wu_ref.at[:, there], sems.at[1, t]),
            pltpu.make_async_copy(down_ref.at[here, :], wd_ref.at[there, :], sems.at[2, t]),
        )

    if opener:
        gk_ref, uk_ref, dk_ref, gm_ref, um_ref, dm_ref, mask_sems = rest
        fetches = [pltpu.make_async_copy(a, b, mask_sems.at[i]) for i, (a, b) in enumerate(zip(keeps, (gm_ref, um_ref, dm_ref)))]
        for fetch in fetches:
            fetch.start()
    else:
        gk_ref, uk_ref, dk_ref = keeps
    for t in range(min(AHEAD, tiles)):
        for copy in copies(t):
            copy.start()
    tok_ref[...] = jnp.zeros_like(tok_ref)
    if opener:
        for fetch in fetches:
            fetch.wait()
        keep_rows(place, gm_ref, um_ref, dm_ref, gk_ref, uk_ref, dk_ref, granule)

    second = place[2] > 0
    x = both_halves([both_ref[0]], half, second)
    og = both_halves([both_ref[1]], half, second)

    def put(k, t, part):
        here = pl.ds(t * tile, tile)
        keep_ref[k, :, here] = part[:half]
        for ks, ref in zip(pieces, sends):
            if k in ks:
                ref[ks.index(k), :, here] = part[half:]

    for t in range(tiles):
        here, lanes = pl.ds(t * tile, tile), pl.ds((first + t) * tile, tile)
        arrivals = copies(t)
        for k, (w_ref, r_ref) in enumerate(((wg_ref, gk_ref), (wu_ref, uk_ref))):
            arrivals[k].wait()
            if t + AHEAD < tiles:
                copies(t + AHEAD)[k].start()
            weight = mask_rows(w_ref[:, here], r_ref[:, lanes], BLK)
            w_ref[:, here] = weight
            put(k, t, jnp.dot(x, weight, preferred_element_type=F32).astype(BF))
        arrivals[2].wait()
        if t + AHEAD < tiles:
            copies(t + AHEAD)[2].start()
        masks = pl.ds((first + t) * granules * LANE, granules * LANE)
        weight = mask_rows(wd_ref[here, :], dk_ref[masks, :], granule)
        wd_ref[here, :] = weight
        put(2, t, dot_nt(og, weight).astype(BF))


def keep_rows(place, gm_ref, um_ref, dm_ref, gk_ref, uk_ref, dk_ref, granule):
    feat_block, unit_first = place[0], place[1]
    n_feat, n_unit = gm_ref.shape
    units, feats = gk_ref.shape[1], dk_ref.shape[1]
    iota = lax.broadcasted_iota
    rows = (feats // BLK * LANE, n_feat)
    rows = one_hot(rows, iota(jnp.int32, rows, 1) == feat_block + iota(jnp.int32, rows, 0) // LANE)
    lanes = (n_unit, units)
    lanes = one_hot(lanes, iota(jnp.int32, lanes, 0) == (unit_first + iota(jnp.int32, lanes, 1)) // BLK)
    for m_ref, r_ref in ((gm_ref, gk_ref), (um_ref, uk_ref)):
        picked = jnp.dot(rows, live(m_ref), preferred_element_type=F32).astype(BF)
        r_ref[...] = jnp.dot(picked, lanes, preferred_element_type=F32).astype(BF)
    rows = (units // granule * LANE, n_unit)
    rows = one_hot(rows, iota(jnp.int32, rows, 1) == (unit_first + iota(jnp.int32, rows, 0) // LANE * granule) // BLK)
    lanes = (n_feat, feats)
    lanes = one_hot(lanes, iota(jnp.int32, lanes, 0) == feat_block + iota(jnp.int32, lanes, 1) // BLK)
    picked = dot_nt(rows, live(dm_ref)).astype(BF)
    dk_ref[...] = jnp.dot(picked, lanes, preferred_element_type=F32).astype(BF)


TOKEN = jax.ShapeDtypeStruct((8, 128), F32)


def open_weights(place, both, gate_w, up_w, down_w, masks, keeps, first, tiles, tile, granule, pieces, deps):
    _, rows, feats = both.shape
    units = gate_w.shape[1]
    half = rows // 2
    span = tiles * tile
    opener = keeps is None
    made = [
        jax.ShapeDtypeStruct((feats // BLK * LANE, units), BF),
        jax.ShapeDtypeStruct((feats // BLK * LANE, units), BF),
        jax.ShapeDtypeStruct((units // granule * LANE, feats), BF),
    ]
    scratch = [pltpu.VMEM(m.shape, m.dtype) for m in masks] + [pltpu.SemaphoreType.DMA((3,))]
    keep, *rest = pl.pallas_call(
        functools.partial(open_kernel, len(deps), pieces, opener, first, tiles, tile, granule),
        out_shape=(
            jax.ShapeDtypeStruct((3, half, span), BF),
            *[jax.ShapeDtypeStruct((len(ks), half, span), BF) for ks in pieces],
            pltpu.VMEM((feats, span), BF),
            pltpu.VMEM((feats, span), BF),
            pltpu.VMEM((span, feats), BF),
            TOKEN,
            *(made if opener else ()),
        ),
        in_specs=[SMEM, VMEM, ANY, ANY, ANY] + [ANY if opener else VMEM] * 3 + [ANY] * len(deps),
        out_specs=[VMEM] * (5 + len(pieces) + (3 if opener else 0)),
        scratch_shapes=(scratch if opener else []) + [pltpu.SemaphoreType.DMA((3, tiles))],
        compiler_params=params(),
        cost_estimate=cost(6 * rows * feats * span, 6 * feats * span),
        name="open_weights",
    )(place, both, *map(in_hbm, (gate_w, up_w, down_w)), *(map(in_hbm, masks) if opener else keeps), *deps)
    n = len(pieces)
    return keep, rest[:n], rest[n : n + 3], rest[n + 4 :] if opener else keeps


def forward_kernel(pieces, own, offset, span, x_ref, og_ref, wg_ref, wu_ref, wd_ref, *rest):
    keep_ref, *sends, tok_ref = rest[-2 - len(pieces) :]
    half = keep_ref.shape[1]
    tok_ref[...] = jnp.zeros_like(tok_ref)
    x = x_ref[own:, :]
    here = pl.ds(offset, span)

    def put(k, value):
        value = value.astype(BF)
        keep_ref[k] = value[:half]
        for ks, ref in zip(pieces, sends):
            if k in ks:
                ref[ks.index(k)] = value[half:]

    put(0, jnp.dot(x, wg_ref[:, here], preferred_element_type=F32))
    put(1, jnp.dot(x, wu_ref[:, here], preferred_element_type=F32))
    put(2, dot_nt(og_ref[own:, :], wd_ref[here, :]))


def forward(x_all, og_all, own, wg, wu, wd, offset, span, pieces, deps):
    rows, feats = x_all.shape[0] - own, x_all.shape[1]
    keep, *sends, tok = pl.pallas_call(
        functools.partial(forward_kernel, pieces, own, offset, span),
        out_shape=(
            jax.ShapeDtypeStruct((3, rows // 2, span), BF),
            *[jax.ShapeDtypeStruct((len(ks), rows // 2, span), BF) for ks in pieces],
            TOKEN,
        ),
        in_specs=[VMEM] * 5 + [ANY] * len(deps),
        out_specs=[VMEM] * (2 + len(pieces)),
        compiler_params=params(),
        cost_estimate=cost(6 * rows * feats * span, 6 * feats * span),
        name="forward",
    )(x_all, og_all, in_vmem(wg), in_vmem(wu), in_vmem(wd), *deps)
    return keep, sends, tok


def tokens_kernel(n_far, own, place, both_ref, *rest):
    refs = rest[:n_far]
    x_ref, xt_ref, og_ref, tok_ref = rest[-4:]
    second = place[2] > 0
    tok_ref[...] = jnp.zeros_like(tok_ref)
    half = own // 2
    for k, out_ref in ((0, x_ref), (1, og_ref)):
        whole = jnp.concatenate(
            [both_halves([both_ref[k]], half, second), both_halves(far_blocks(refs, k, own), half, second)], axis=0
        )
        out_ref[...] = whole
        if k == 0:
            xt_ref[...] = whole.T


def all_tokens(place, both, far, deps):
    _, own, feats = both.shape
    rows = own + sum(f.shape[1] for f in far)
    return pl.pallas_call(
        functools.partial(tokens_kernel, len(far), own),
        out_shape=(
            jax.ShapeDtypeStruct((rows, feats), BF),
            jax.ShapeDtypeStruct((feats, rows), BF),
            jax.ShapeDtypeStruct((rows, feats), BF),
            TOKEN,
        ),
        in_specs=[SMEM] + [VMEM] * (1 + len(far)) + [ANY] * len(deps),
        out_specs=[VMEM] * 4,
        compiler_params=params(),
        cost_estimate=cost(rows * feats, 8 * rows * feats),
        name="all_tokens",
    )(place, both, *far, *deps)


def sum_kernel(pieces, keep_ref, *rest):
    others, out_ref = rest[: len(pieces)], rest[-1]
    for ks, other in zip(pieces, others):
        for i, k in enumerate(ks):
            out_ref[k] = (keep_ref[k].astype(F32) + other[i].astype(F32)).astype(BF)


def sum_of(keep, others, pieces, deps):
    return pl.pallas_call(
        functools.partial(sum_kernel, pieces),
        out_shape=jax.ShapeDtypeStruct(keep.shape, BF),
        in_specs=[VMEM] * (1 + len(others)) + [ANY] * len(deps),
        out_specs=VMEM,
        compiler_params=params(),
        cost_estimate=cost(keep.size, 6 * keep.size),
        name="sum_cores",
    )(keep, *others, *deps)


def pointwise_kernel(n_other, sum_ref, *rest):
    others, (hidden_ref, gate_ref, up_ref, tok_ref) = rest[:n_other], rest[-4:]
    rows = hidden_ref.shape[0]
    tok_ref[...] = jnp.zeros_like(tok_ref)

    def step(here):
        total = [sum_ref[k, here, :].astype(F32) for k in range(3)]
        for other in others:
            total = [total[k] + other[k, here, :].astype(F32) for k in range(3)]
        gate_pre, up_pre, hidden_grad = total
        sigmoid_gate = jax.nn.sigmoid(gate_pre)
        active = gate_pre * sigmoid_gate
        hidden_ref[here, :] = (active * up_pre).astype(BF)
        gate_ref[here, :] = (
            hidden_grad * up_pre * sigmoid_gate * (1.0 + gate_pre * (1.0 - sigmoid_gate))
        ).astype(BF)
        up_ref[here, :] = (hidden_grad * active).astype(BF)

    if rows == 16:
        step(pl.ds(0, rows))
    else:

        @pl.loop(0, rows // 16)
        def _(i):
            step(pl.ds(pl.multiple_of(i * 16, 16), 16))


def pointwise(chip_sum, others, deps):
    return pl.pallas_call(
        functools.partial(pointwise_kernel, len(others)),
        out_shape=(*[jax.ShapeDtypeStruct(chip_sum.shape[1:], BF)] * 3, TOKEN),
        in_specs=[VMEM] * (1 + len(others)) + [ANY] * len(deps),
        out_specs=[VMEM] * 4,
        compiler_params=params(),
        cost_estimate=cost(20 * chip_sum.size, 6 * chip_sum.size),
        name="pointwise",
    )(chip_sum, *others, *deps)


def grad_tokens_kernel(offsets, weight_offset, span, own, n_out, prev_ref, wg_ref, wu_ref, *rest):
    n = len(offsets)
    gates, ups, (*outs, tok_ref) = rest[:n], rest[n : 2 * n], rest[-1 - n_out :]
    tok_ref[...] = jnp.zeros_like(tok_ref)
    here = pl.ds(weight_offset, span)
    gate_act = jnp.concatenate([p[:, s : s + span] for p, s in zip(gates, offsets)], axis=0)
    up_act = jnp.concatenate([p[:, s : s + span] for p, s in zip(ups, offsets)], axis=0)
    add = dot_nt(gate_act, wg_ref[:, here]) + dot_nt(up_act, wu_ref[:, here])
    if prev_ref is not None:
        add += prev_ref[...]
    if not own:
        outs[0][...] = add
        return
    half = own // 2
    blocks = outs[0].shape[0] // own
    outs[1][...] = add[:own]
    add = add.astype(BF)
    for b in range(blocks):
        for h in range(2):
            start = own + (h * blocks + b) * half
            outs[0][pl.ds(b * own + h * half, half), :] = add[start : start + half]


def grad_tokens_of(prev, wg, wu, weight_offset, parts, offsets, span, own, deps):
    rows = sum(p[1].shape[0] for p in parts)
    feats = wg.shape[0]
    outs = [jax.ShapeDtypeStruct((rows, feats), F32)]
    if own:
        outs = [jax.ShapeDtypeStruct((rows - own, feats), BF), jax.ShapeDtypeStruct((own, feats), F32)]
    kernel = functools.partial(grad_tokens_kernel, offsets, weight_offset, span, own, len(outs))
    prevs = (prev,)
    if prev is None:
        kernel, prevs = functools.partial(kernel, None), ()
    return pl.pallas_call(
        kernel,
        out_shape=(*outs, TOKEN),
        in_specs=[VMEM] * (len(prevs) + 2 + 2 * len(parts)) + [ANY] * len(deps),
        out_specs=[VMEM] * (1 + len(outs)),
        compiler_params=params(),
        cost_estimate=cost(4 * rows * feats * span, 4 * feats * span),
        name="grad_tokens",
    )(*prevs, in_vmem(wg), in_vmem(wu), *[p[1] for p in parts], *[p[2] for p in parts], *deps)


def weight_grads_kernel(n, granule, xt_ref, og_ref, gk_ref, uk_ref, dk_ref, *rest):
    gate_ref, up_ref, down_ref, tok_ref = rest[-4:]
    tok_ref[...] = jnp.zeros_like(tok_ref)
    hidden, gate_act, up_act = [
        jnp.concatenate([p[...] for p in rest[k * n : (k + 1) * n]], axis=0) for k in range(3)
    ]
    for act, keep, out_ref in ((gate_act, gk_ref, gate_ref), (up_act, uk_ref, up_ref)):
        value = jnp.dot(xt_ref[...], act, preferred_element_type=F32).astype(BF)
        out_ref[...] = mask_rows(value, keep[...], BLK)
    down_ref[...] = mask_rows(dot_tn(hidden, og_ref[...]).astype(BF), dk_ref[...], granule)


def weight_grads(prev, xt, og, gk, uk, dk, weight_start, parts, starts, first, tiles, tile, units, granule, deps):
    feats, rows = xt.shape
    span = tiles * tile
    n_prev = 0 if prev is None else 3
    base = 5 + 3 * len(parts)

    def moved(s, i):
        return (0, s + i)

    return pl.pallas_call(
        functools.partial(weight_grads_kernel, len(parts), granule),
        out_shape=(
            pltpu.HBM((feats, units), BF),
            pltpu.HBM((feats, units), BF),
            pltpu.HBM((units, feats), BF),
            TOKEN,
        ),
        grid=(tiles,),
        in_specs=[
            pl.BlockSpec((feats, rows), lambda i: (0, 0)),
            pl.BlockSpec((rows, feats), lambda i: (0, 0)),
            pl.BlockSpec((gk.shape[0], tile), lambda i: (0, weight_start + i)),
            pl.BlockSpec((uk.shape[0], tile), lambda i: (0, weight_start + i)),
            pl.BlockSpec((tile // granule * LANE, feats), lambda i: (weight_start + i, 0)),
        ]
        + [pl.BlockSpec((p[0].shape[0], tile), functools.partial(moved, s)) for p, s in zip(parts, starts)] * 3
        + [ANY] * (n_prev + len(deps)),
        out_specs=[
            pl.BlockSpec((feats, tile), lambda i: (0, first + i)),
            pl.BlockSpec((feats, tile), lambda i: (0, first + i)),
            pl.BlockSpec((tile, feats), lambda i: (first + i, 0)),
            pl.BlockSpec((8, 128), lambda i: (0, 0)),
        ],
        input_output_aliases={base + k: k for k in range(n_prev)},
        compiler_params=params(16),
        cost_estimate=cost(6 * rows * feats * span, 6 * feats * span),
        name="weight_grads",
    )(xt, og, gk, uk, dk, *[p[k] for k in range(3) for p in parts], *(() if prev is None else map(in_hbm, prev)), *deps)


def finish_kernel(place, own_ref, *rest):
    arrived, out_ref = rest[:-1], rest[-1]
    total = own_ref[...]
    for piece in arrived:
        total += piece[...].astype(F32)
    out_ref[...] = both_halves([total.astype(BF)], total.shape[0] // 2, place[2] > 0)


def finish(place, own, arrived):
    return pl.pallas_call(
        finish_kernel,
        out_shape=jax.ShapeDtypeStruct(own.shape, BF),
        in_specs=[SMEM] + [VMEM] * (1 + len(arrived)),
        out_specs=VMEM,
        compiler_params=params(),
        cost_estimate=cost(4 * own.size, 8 * own.size),
        name="finish",
    )(place, own, *arrived)


def chunks_of(tiles, sizes):
    out, first = [], 0
    for size in sizes:
        size = min(size, tiles - first)
        if size > 0:
            out.append((first, size))
            first += size
    if first < tiles:
        out.append((first, tiles - first))
    return out


def local(n_row, n_col, tokens, out_grad, gate_w, up_w, down_w, gate_mask, up_mask, down_mask):
    rank_row, rank_col = lax.axis_index("row"), lax.axis_index("col")
    own, feats = tokens.shape
    units = gate_w.shape[1]
    half = own // 2
    n_chip = n_col // 2
    tile = TILE if units % TILE == 0 else units
    tiles = units // tile
    granule = gcd_of(units, BLK)
    core_swap = [(i, i ^ 1) for i in range(n_col)]

    def swap_cores(values):
        return [lax.ppermute(value, "col", core_swap) for value in values]

    def flipped(value, d):
        return lax.ppermute(value, "row", [(i, i ^ d) for i in range(n_row)])

    def from_chips(value):
        return [
            lax.ppermute(value, "col", [(i, (i + 2 * d) % n_col) for i in range(n_col)])
            for d in range(1, n_chip)
        ]

    both = jnp.stack([tokens, out_grad])
    if n_row == 4:
        two = flipped(both, 2)
        far = [flipped(both, 1), two, flipped(two, 1)]
    else:
        whole = lax.all_gather(both, "row", axis=1, tiled=True)
        wanted = [rank_row ^ d for d in range(1, n_row)]
        far = [jnp.concatenate([lax.dynamic_slice_in_dim(whole, w * own, own, 1) for w in wanted], axis=1)]

    place = jnp.stack([rank_col * (feats // BLK), rank_row * units, rank_col % 2]).astype(jnp.int32)
    masks = (gate_mask, up_mask, down_mask.T)

    own_chunks = chunks_of(tiles, OWN_CHUNKS)
    far_chunks = chunks_of(tiles, FAR_CHUNKS)

    def group_of(first):
        for g, (f, s) in enumerate(own_chunks):
            if f <= first < f + s:
                return g, first - f

    groups, own_sums, own_others, keeps, deps = [], [], [], None, ()
    for c, (first, size) in enumerate(own_chunks):
        pieces = OWN_PIECES[min(c, len(OWN_PIECES) - 1)]
        keep, send, group, keeps = open_weights(
            place, both, gate_w, up_w, down_w, masks, keeps, first, size, tile, granule, pieces, deps
        )
        groups.append(group)
        own_sums.append(sum_of(keep, swap_cores(send), pieces, ()))
        own_others.append(from_chips(own_sums[-1]))
        deps = (own_sums[-1],)

    x_all, xt_all, og_all, tok = all_tokens(place, both, far, deps)
    deps = (tok,)
    far_sums, far_others, own_parts, waiting = [], [], [], None

    def open_own(c, deps):
        *mine, tok = pointwise(own_sums[c], own_others[c], deps)
        own_parts.append((mine, swap_cores(mine)))
        return (tok,)

    for first, size in far_chunks:
        g, offset = group_of(first)
        keep, send, tok = forward(x_all, og_all, own, *groups[g], offset * tile, size * tile, FAR_PIECES, deps)
        deps = (tok,)
        if waiting is not None:
            far_sums.append(sum_of(*waiting, FAR_PIECES, far_sums[-1:]))
            far_others.append(from_chips(far_sums[-1]))
            deps += (far_sums[-1],)
        waiting = (keep, swap_cores(send))
        if len(own_parts) < len(own_chunks) and len(far_sums) >= OWN_AFTER[len(own_parts)]:
            deps = open_own(len(own_parts), deps)
    far_sums.append(sum_of(*waiting, FAR_PIECES, far_sums[-1:]))
    far_others.append(from_chips(far_sums[-1]))

    deps = (far_sums[-1],)
    while len(own_parts) < len(own_chunks):
        deps = open_own(len(own_parts), deps)

    grads, gt, pending = None, None, []

    def flush(grads, work, deps):
        first, size, g, offset, parts, starts = work
        *grads, tok = weight_grads(
            grads, xt_all, og_all, *keeps, first, parts, starts, first, size, tile, units, granule, deps
        )
        return grads, (tok,)

    for c, (first, size) in enumerate(far_chunks):
        g, offset = group_of(first)
        *mine, tok = pointwise(far_sums[c], far_others[c], deps)
        deps = (tok,)
        parts = (*own_parts[g], mine, swap_cores(mine))
        last = c == len(far_chunks) - 1
        if pending and not (last and DEFER):
            grads, deps = flush(grads, pending.pop(0), deps)
        offsets = (offset * tile, offset * tile, 0, 0)
        gt, *rest, tok = grad_tokens_of(
            gt, *groups[g][:2], offset * tile, parts, offsets, size * tile, own if last else 0, deps
        )
        deps = (tok,)
        pending.append((first, size, g, offset, parts, (offset, offset, 0, 0)))
    for work in pending:
        grads, deps = flush(grads, work, deps)

    if n_row == 4:
        arrived = [flipped(gt[(d - 1) * own : d * own], d) for d in range(1, n_row)]
    else:
        blocks = jnp.concatenate([rest[0].astype(BF), gt], axis=0).reshape(n_row, own, feats)
        wanted = [rank_row ^ b for b in range(n_row)]
        by_row = jnp.concatenate([lax.dynamic_slice_in_dim(blocks, w, 1, 0) for w in wanted], axis=0)
        arrived = [lax.psum_scatter(by_row.reshape(n_row * own, feats), "row", scatter_dimension=0, tiled=True)]
        rest = [jnp.zeros_like(rest[0])]
    return (finish(place, rest[0], arrived), *grads)


def solution(mesh):
    in_specs = (
        P(("groups", "row"), "col"),
        P(("groups", "row"), "col"),
        P(("groups", "col"), "row"),
        P(("groups", "col"), "row"),
        P(("groups", "row"), "col"),
        P("groups", None),
        P("groups", None),
        P("groups", None),
    )
    out_specs = (
        P(("groups", "row"), "col"),
        P(("groups", "col"), "row"),
        P(("groups", "col"), "row"),
        P(("groups", "row"), "col"),
    )
    step = functools.partial(local, mesh.shape["row"], mesh.shape["col"])
    return jax.shard_map(step, mesh=mesh, in_specs=in_specs, out_specs=out_specs, check_vma=False)
```

```python
import functools

import jax
import jax.numpy as jnp
from jax import lax
from jax.experimental import pallas as pl
from jax.experimental.pallas import tpu as pltpu
from jax.sharding import PartitionSpec as P

BLK = 128
TILE = 512
LANE = 16
AHEAD = 2
COST_SCALE = 1000000000
OWN_CHUNKS = (4, 3)
OWN_PIECES = (((0,), (1,), (2,)), ((0, 1), (2,)))
OWN_AFTER = (1, 2)
DEFER = True
FAR_PIECES = ((0,), (1,), (2,))
FAR_CHUNKS = (2, 2, 2, 1)
BF = jnp.bfloat16
F32 = jnp.float32
ANY = pl.BlockSpec(memory_space=pl.ANY)
VMEM = pl.BlockSpec(memory_space=pltpu.VMEM)
SMEM = pl.BlockSpec(memory_space=pltpu.SMEM)


def params(mib=8):
    return pltpu.CompilerParams(vmem_limit_bytes=mib * 1024 * 1024)


def cost(flops, nbytes):
    return pl.CostEstimate(flops=int(flops) // COST_SCALE, bytes_accessed=int(nbytes) // COST_SCALE, transcendentals=0)


def gcd_of(a, b):
    while b:
        a, b = b, a % b
    return a


def in_vmem(value):
    return pltpu.with_memory_space_constraint(value, pltpu.VMEM)


def in_hbm(value):
    return pltpu.with_memory_space_constraint(value, pltpu.HBM)


def mask_rows(weight, keep, rows):
    pieces = []
    for i in range(weight.shape[0] // rows):
        mask = keep[LANE * i : LANE * (i + 1), :]
        pieces += [weight[i * rows + g : i * rows + g + LANE, :] * mask for g in range(0, rows, LANE)]
    return jnp.concatenate(pieces, axis=0)


def dot_nt(left, right):
    return lax.dot_general(left, right, (((1,), (1,)), ((), ())), preferred_element_type=F32)


def dot_tn(left, right):
    return lax.dot_general(left, right, (((0,), (0,)), ((), ())), preferred_element_type=F32)


def both_halves(blocks, half, second):
    low = [b[:half] for b in blocks]
    high = [b[half:] for b in blocks]
    mine = [jnp.where(second, h, l) for l, h in zip(low, high)]
    theirs = [jnp.where(second, l, h) for l, h in zip(low, high)]
    return jnp.concatenate(mine + theirs, axis=0)


def far_blocks(refs, k, own):
    return [r[k, b * own : (b + 1) * own, :] for r in refs for b in range(r.shape[1] // own)]


def one_hot(shape, match):
    return jnp.where(match, jnp.ones(shape, F32), jnp.zeros(shape, F32)).astype(BF)


def live(mask_ref):
    return jnp.where(mask_ref[...] > 0, 1.0, 0.0).astype(BF)


def open_kernel(n_deps, pieces, opener, first, tiles, tile, granule, place, both_ref, gate_ref, up_ref, down_ref, *rest):
    keeps, rest = rest[:3], rest[3 + n_deps :]
    keep_ref, *sends = rest[: 1 + len(pieces)]
    rest = rest[1 + len(pieces) :]
    wg_ref, wu_ref, wd_ref, tok_ref = rest[:4]
    sems, rest = rest[-1], rest[4:-1]
    half, feats = keep_ref.shape[1], wg_ref.shape[0]
    granules = tile // granule

    def copies(t):
        here, there = pl.ds((first + t) * tile, tile), pl.ds(t * tile, tile)
        return (
            pltpu.make_async_copy(gate_ref.at[:, here], wg_ref.at[:, there], sems.at[0, t]),
            pltpu.make_async_copy(up_ref.at[:, here], wu_ref.at[:, there], sems.at[1, t]),
            pltpu.make_async_copy(down_ref.at[here, :], wd_ref.at[there, :], sems.at[2, t]),
        )

    if opener:
        gk_ref, uk_ref, dk_ref, gm_ref, um_ref, dm_ref, mask_sems = rest
        fetches = [pltpu.make_async_copy(a, b, mask_sems.at[i]) for i, (a, b) in enumerate(zip(keeps, (gm_ref, um_ref, dm_ref)))]
        for fetch in fetches:
            fetch.start()
    else:
        gk_ref, uk_ref, dk_ref = keeps
    for t in range(min(AHEAD, tiles)):
        for copy in copies(t):
            copy.start()
    tok_ref[...] = jnp.zeros_like(tok_ref)
    if opener:
        for fetch in fetches:
            fetch.wait()
        keep_rows(place, gm_ref, um_ref, dm_ref, gk_ref, uk_ref, dk_ref, granule)

    second = place[2] > 0
    x = both_halves([both_ref[0]], half, second)
    og = both_halves([both_ref[1]], half, second)

    def put(k, t, part):
        here = pl.ds(t * tile, tile)
        keep_ref[k, :, here] = part[:half]
        for ks, ref in zip(pieces, sends):
            if k in ks:
                ref[ks.index(k), :, here] = part[half:]

    for t in range(tiles):
        here, lanes = pl.ds(t * tile, tile), pl.ds((first + t) * tile, tile)
        arrivals = copies(t)
        for k, (w_ref, r_ref) in enumerate(((wg_ref, gk_ref), (wu_ref, uk_ref))):
            arrivals[k].wait()
            if t + AHEAD < tiles:
                copies(t + AHEAD)[k].start()
            weight = mask_rows(w_ref[:, here], r_ref[:, lanes], BLK)
            w_ref[:, here] = weight
            put(k, t, jnp.dot(x, weight, preferred_element_type=F32).astype(BF))
        arrivals[2].wait()
        if t + AHEAD < tiles:
            copies(t + AHEAD)[2].start()
        masks = pl.ds((first + t) * granules * LANE, granules * LANE)
        weight = mask_rows(wd_ref[here, :], dk_ref[masks, :], granule)
        wd_ref[here, :] = weight
        put(2, t, dot_nt(og, weight).astype(BF))


def keep_rows(place, gm_ref, um_ref, dm_ref, gk_ref, uk_ref, dk_ref, granule):
    feat_block, unit_first = place[0], place[1]
    n_feat, n_unit = gm_ref.shape
    units, feats = gk_ref.shape[1], dk_ref.shape[1]
    iota = lax.broadcasted_iota
    rows = (feats // BLK * LANE, n_feat)
    rows = one_hot(rows, iota(jnp.int32, rows, 1) == feat_block + iota(jnp.int32, rows, 0) // LANE)
    lanes = (n_unit, units)
    lanes = one_hot(lanes, iota(jnp.int32, lanes, 0) == (unit_first + iota(jnp.int32, lanes, 1)) // BLK)
    for m_ref, r_ref in ((gm_ref, gk_ref), (um_ref, uk_ref)):
        picked = jnp.dot(rows, live(m_ref), preferred_element_type=F32).astype(BF)
        r_ref[...] = jnp.dot(picked, lanes, preferred_element_type=F32).astype(BF)
    rows = (units // granule * LANE, n_unit)
    rows = one_hot(rows, iota(jnp.int32, rows, 1) == (unit_first + iota(jnp.int32, rows, 0) // LANE * granule) // BLK)
    lanes = (n_feat, feats)
    lanes = one_hot(lanes, iota(jnp.int32, lanes, 0) == feat_block + iota(jnp.int32, lanes, 1) // BLK)
    picked = dot_nt(rows, live(dm_ref)).astype(BF)
    dk_ref[...] = jnp.dot(picked, lanes, preferred_element_type=F32).astype(BF)


TOKEN = jax.ShapeDtypeStruct((8, 128), F32)


def open_weights(place, both, gate_w, up_w, down_w, masks, keeps, first, tiles, tile, granule, pieces, deps):
    _, rows, feats = both.shape
    units = gate_w.shape[1]
    half = rows // 2
    span = tiles * tile
    opener = keeps is None
    made = [
        jax.ShapeDtypeStruct((feats // BLK * LANE, units), BF),
        jax.ShapeDtypeStruct((feats // BLK * LANE, units), BF),
        jax.ShapeDtypeStruct((units // granule * LANE, feats), BF),
    ]
    scratch = [pltpu.VMEM(m.shape, m.dtype) for m in masks] + [pltpu.SemaphoreType.DMA((3,))]
    keep, *rest = pl.pallas_call(
        functools.partial(open_kernel, len(deps), pieces, opener, first, tiles, tile, granule),
        out_shape=(
            jax.ShapeDtypeStruct((3, half, span), BF),
            *[jax.ShapeDtypeStruct((len(ks), half, span), BF) for ks in pieces],
            pltpu.VMEM((feats, span), BF),
            pltpu.VMEM((feats, span), BF),
            pltpu.VMEM((span, feats), BF),
            TOKEN,
            *(made if opener else ()),
        ),
        in_specs=[SMEM, VMEM, ANY, ANY, ANY] + [ANY if opener else VMEM] * 3 + [ANY] * len(deps),
        out_specs=[VMEM] * (5 + len(pieces) + (3 if opener else 0)),
        scratch_shapes=(scratch if opener else []) + [pltpu.SemaphoreType.DMA((3, tiles))],
        compiler_params=params(),
        cost_estimate=cost(6 * rows * feats * span, 6 * feats * span),
        name="open_weights",
    )(place, both, *map(in_hbm, (gate_w, up_w, down_w)), *(map(in_hbm, masks) if opener else keeps), *deps)
    n = len(pieces)
    return keep, rest[:n], rest[n : n + 3], rest[n + 4 :] if opener else keeps


def forward_kernel(pieces, own, offset, span, x_ref, og_ref, wg_ref, wu_ref, wd_ref, *rest):
    keep_ref, *sends, tok_ref = rest[-2 - len(pieces) :]
    half = keep_ref.shape[1]
    tok_ref[...] = jnp.zeros_like(tok_ref)
    x = x_ref[own:, :]
    here = pl.ds(offset, span)

    def put(k, value):
        value = value.astype(BF)
        keep_ref[k] = value[:half]
        for ks, ref in zip(pieces, sends):
            if k in ks:
                ref[ks.index(k)] = value[half:]

    put(0, jnp.dot(x, wg_ref[:, here], preferred_element_type=F32))
    put(1, jnp.dot(x, wu_ref[:, here], preferred_element_type=F32))
    put(2, dot_nt(og_ref[own:, :], wd_ref[here, :]))


def forward(x_all, og_all, own, wg, wu, wd, offset, span, pieces, deps):
    rows, feats = x_all.shape[0] - own, x_all.shape[1]
    keep, *sends, tok = pl.pallas_call(
        functools.partial(forward_kernel, pieces, own, offset, span),
        out_shape=(
            jax.ShapeDtypeStruct((3, rows // 2, span), BF),
            *[jax.ShapeDtypeStruct((len(ks), rows // 2, span), BF) for ks in pieces],
            TOKEN,
        ),
        in_specs=[VMEM] * 5 + [ANY] * len(deps),
        out_specs=[VMEM] * (2 + len(pieces)),
        compiler_params=params(),
        cost_estimate=cost(6 * rows * feats * span, 6 * feats * span),
        name="forward",
    )(x_all, og_all, in_vmem(wg), in_vmem(wu), in_vmem(wd), *deps)
    return keep, sends, tok


def tokens_kernel(n_far, own, place, both_ref, *rest):
    refs = rest[:n_far]
    x_ref, xt_ref, og_ref, tok_ref = rest[-4:]
    second = place[2] > 0
    tok_ref[...] = jnp.zeros_like(tok_ref)
    half = own // 2
    for k, out_ref in ((0, x_ref), (1, og_ref)):
        whole = jnp.concatenate(
            [both_halves([both_ref[k]], half, second), both_halves(far_blocks(refs, k, own), half, second)], axis=0
        )
        out_ref[...] = whole
        if k == 0:
            xt_ref[...] = whole.T


def all_tokens(place, both, far, deps):
    _, own, feats = both.shape
    rows = own + sum(f.shape[1] for f in far)
    return pl.pallas_call(
        functools.partial(tokens_kernel, len(far), own),
        out_shape=(
            jax.ShapeDtypeStruct((rows, feats), BF),
            jax.ShapeDtypeStruct((feats, rows), BF),
            jax.ShapeDtypeStruct((rows, feats), BF),
            TOKEN,
        ),
        in_specs=[SMEM] + [VMEM] * (1 + len(far)) + [ANY] * len(deps),
        out_specs=[VMEM] * 4,
        compiler_params=params(),
        cost_estimate=cost(rows * feats, 8 * rows * feats),
        name="all_tokens",
    )(place, both, *far, *deps)


def sum_kernel(pieces, keep_ref, *rest):
    others, out_ref = rest[: len(pieces)], rest[-1]
    for ks, other in zip(pieces, others):
        for i, k in enumerate(ks):
            out_ref[k] = (keep_ref[k].astype(F32) + other[i].astype(F32)).astype(BF)


def sum_of(keep, others, pieces, deps):
    return pl.pallas_call(
        functools.partial(sum_kernel, pieces),
        out_shape=jax.ShapeDtypeStruct(keep.shape, BF),
        in_specs=[VMEM] * (1 + len(others)) + [ANY] * len(deps),
        out_specs=VMEM,
        compiler_params=params(),
        cost_estimate=cost(keep.size, 6 * keep.size),
        name="sum_cores",
    )(keep, *others, *deps)


def pointwise_kernel(n_other, sum_ref, *rest):
    others, (hidden_ref, gate_ref, up_ref, tok_ref) = rest[:n_other], rest[-4:]
    rows = hidden_ref.shape[0]
    tok_ref[...] = jnp.zeros_like(tok_ref)

    def step(here):
        total = [sum_ref[k, here, :].astype(F32) for k in range(3)]
        for other in others:
            total = [total[k] + other[k, here, :].astype(F32) for k in range(3)]
        gate_pre, up_pre, hidden_grad = total
        sigmoid_gate = jax.nn.sigmoid(gate_pre)
        active = gate_pre * sigmoid_gate
        hidden_ref[here, :] = (active * up_pre).astype(BF)
        gate_ref[here, :] = (
            hidden_grad * up_pre * sigmoid_gate * (1.0 + gate_pre * (1.0 - sigmoid_gate))
        ).astype(BF)
        up_ref[here, :] = (hidden_grad * active).astype(BF)

    if rows == 16:
        step(pl.ds(0, rows))
    else:

        @pl.loop(0, rows // 16)
        def _(i):
            step(pl.ds(pl.multiple_of(i * 16, 16), 16))


def pointwise(chip_sum, others, deps):
    return pl.pallas_call(
        functools.partial(pointwise_kernel, len(others)),
        out_shape=(*[jax.ShapeDtypeStruct(chip_sum.shape[1:], BF)] * 3, TOKEN),
        in_specs=[VMEM] * (1 + len(others)) + [ANY] * len(deps),
        out_specs=[VMEM] * 4,
        compiler_params=params(),
        cost_estimate=cost(20 * chip_sum.size, 6 * chip_sum.size),
        name="pointwise",
    )(chip_sum, *others, *deps)


def grad_tokens_kernel(offsets, weight_offset, span, own, n_out, prev_ref, wg_ref, wu_ref, *rest):
    n = len(offsets)
    gates, ups, (*outs, tok_ref) = rest[:n], rest[n : 2 * n], rest[-1 - n_out :]
    tok_ref[...] = jnp.zeros_like(tok_ref)
    here = pl.ds(weight_offset, span)
    gate_act = jnp.concatenate([p[:, s : s + span] for p, s in zip(gates, offsets)], axis=0)
    up_act = jnp.concatenate([p[:, s : s + span] for p, s in zip(ups, offsets)], axis=0)
    add = dot_nt(gate_act, wg_ref[:, here]) + dot_nt(up_act, wu_ref[:, here])
    if prev_ref is not None:
        add += prev_ref[...]
    if not own:
        outs[0][...] = add
        return
    half = own // 2
    blocks = outs[0].shape[0] // own
    outs[1][...] = add[:own]
    add = add.astype(BF)
    for b in range(blocks):
        for h in range(2):
            start = own + (h * blocks + b) * half
            outs[0][pl.ds(b * own + h * half, half), :] = add[start : start + half]


def grad_tokens_of(prev, wg, wu, weight_offset, parts, offsets, span, own, deps):
    rows = sum(p[1].shape[0] for p in parts)
    feats = wg.shape[0]
    outs = [jax.ShapeDtypeStruct((rows, feats), F32)]
    if own:
        outs = [jax.ShapeDtypeStruct((rows - own, feats), BF), jax.ShapeDtypeStruct((own, feats), F32)]
    kernel = functools.partial(grad_tokens_kernel, offsets, weight_offset, span, own, len(outs))
    prevs = (prev,)
    if prev is None:
        kernel, prevs = functools.partial(kernel, None), ()
    return pl.pallas_call(
        kernel,
        out_shape=(*outs, TOKEN),
        in_specs=[VMEM] * (len(prevs) + 2 + 2 * len(parts)) + [ANY] * len(deps),
        out_specs=[VMEM] * (1 + len(outs)),
        compiler_params=params(),
        cost_estimate=cost(4 * rows * feats * span, 4 * feats * span),
        name="grad_tokens",
    )(*prevs, in_vmem(wg), in_vmem(wu), *[p[1] for p in parts], *[p[2] for p in parts], *deps)


def weight_grads_kernel(n, n_own, begins, granule, xt_ref, og_ref, gk_ref, uk_ref, dk_ref, *rest):
    gate_ref, up_ref, down_ref, tok_ref = rest[-4:]
    tok_ref[...] = jnp.zeros_like(tok_ref)
    acts = []
    for k in range(3):
        refs = rest[k * n : (k + 1) * n]
        pieces = [p[...] for p in refs[:n_own]]
        for j in range(2):
            piece = refs[n_own + j][...]
            for w in range(1, len(begins)):
                piece = jnp.where(pl.program_id(0) >= begins[w], refs[n_own + 2 * w + j][...], piece)
            pieces.append(piece)
        acts.append(jnp.concatenate(pieces, axis=0))
    hidden, gate_act, up_act = acts
    for act, keep, out_ref in ((gate_act, gk_ref, gate_ref), (up_act, uk_ref, up_ref)):
        value = jnp.dot(xt_ref[...], act, preferred_element_type=F32).astype(BF)
        out_ref[...] = mask_rows(value, keep[...], BLK)
    down_ref[...] = mask_rows(dot_tn(hidden, og_ref[...]).astype(BF), dk_ref[...], granule)


def weight_grads(prev, xt, og, gk, uk, dk, weight_start, parts, maps, begins, first, tiles, tile, units, granule, deps):
    feats, rows = xt.shape
    span = tiles * tile
    n_prev = 0 if prev is None else 3
    base = 5 + 3 * len(parts)

    def moved(s, least, most, i):
        return (0, jnp.clip(s + i, least, most))

    return pl.pallas_call(
        functools.partial(weight_grads_kernel, len(parts), 2, begins, granule),
        out_shape=(
            pltpu.HBM((feats, units), BF),
            pltpu.HBM((feats, units), BF),
            pltpu.HBM((units, feats), BF),
            TOKEN,
        ),
        grid=(tiles,),
        in_specs=[
            pl.BlockSpec((feats, rows), lambda i: (0, 0)),
            pl.BlockSpec((rows, feats), lambda i: (0, 0)),
            pl.BlockSpec((gk.shape[0], tile), lambda i: (0, weight_start + i)),
            pl.BlockSpec((uk.shape[0], tile), lambda i: (0, weight_start + i)),
            pl.BlockSpec((tile // granule * LANE, feats), lambda i: (weight_start + i, 0)),
        ]
        + [pl.BlockSpec((p[0].shape[0], tile), functools.partial(moved, *m)) for p, m in zip(parts, maps)] * 3
        + [ANY] * (n_prev + len(deps)),
        out_specs=[
            pl.BlockSpec((feats, tile), lambda i: (0, first + i)),
            pl.BlockSpec((feats, tile), lambda i: (0, first + i)),
            pl.BlockSpec((tile, feats), lambda i: (first + i, 0)),
            pl.BlockSpec((8, 128), lambda i: (0, 0)),
        ],
        input_output_aliases={base + k: k for k in range(n_prev)},
        compiler_params=params(16),
        cost_estimate=cost(6 * rows * feats * span, 6 * feats * span),
        name="weight_grads",
    )(xt, og, gk, uk, dk, *[p[k] for k in range(3) for p in parts], *(() if prev is None else map(in_hbm, prev)), *deps)


def finish_kernel(place, own_ref, *rest):
    arrived, out_ref = rest[:-1], rest[-1]
    total = own_ref[...]
    for piece in arrived:
        total += piece[...].astype(F32)
    out_ref[...] = both_halves([total.astype(BF)], total.shape[0] // 2, place[2] > 0)


def finish(place, own, arrived):
    return pl.pallas_call(
        finish_kernel,
        out_shape=jax.ShapeDtypeStruct(own.shape, BF),
        in_specs=[SMEM] + [VMEM] * (1 + len(arrived)),
        out_specs=VMEM,
        compiler_params=params(),
        cost_estimate=cost(4 * own.size, 8 * own.size),
        name="finish",
    )(place, own, *arrived)


def chunks_of(tiles, sizes):
    out, first = [], 0
    for size in sizes:
        size = min(size, tiles - first)
        if size > 0:
            out.append((first, size))
            first += size
    if first < tiles:
        out.append((first, tiles - first))
    return out


def local(n_row, n_col, tokens, out_grad, gate_w, up_w, down_w, gate_mask, up_mask, down_mask):
    rank_row, rank_col = lax.axis_index("row"), lax.axis_index("col")
    own, feats = tokens.shape
    units = gate_w.shape[1]
    half = own // 2
    n_chip = n_col // 2
    tile = TILE if units % TILE == 0 else units
    tiles = units // tile
    granule = gcd_of(units, BLK)
    core_swap = [(i, i ^ 1) for i in range(n_col)]

    def swap_cores(values):
        return [lax.ppermute(value, "col", core_swap) for value in values]

    def flipped(value, d):
        return lax.ppermute(value, "row", [(i, i ^ d) for i in range(n_row)])

    def from_chips(value):
        return [
            lax.ppermute(value, "col", [(i, (i + 2 * d) % n_col) for i in range(n_col)])
            for d in range(1, n_chip)
        ]

    both = jnp.stack([tokens, out_grad])
    if n_row == 4:
        two = flipped(both, 2)
        far = [flipped(both, 1), two, flipped(two, 1)]
    else:
        whole = lax.all_gather(both, "row", axis=1, tiled=True)
        wanted = [rank_row ^ d for d in range(1, n_row)]
        far = [jnp.concatenate([lax.dynamic_slice_in_dim(whole, w * own, own, 1) for w in wanted], axis=1)]

    place = jnp.stack([rank_col * (feats // BLK), rank_row * units, rank_col % 2]).astype(jnp.int32)
    masks = (gate_mask, up_mask, down_mask.T)

    own_chunks = chunks_of(tiles, OWN_CHUNKS)
    far_chunks = chunks_of(tiles, FAR_CHUNKS)

    def group_of(first):
        for g, (f, s) in enumerate(own_chunks):
            if f <= first < f + s:
                return g, first - f

    groups, own_sums, own_others, keeps, deps = [], [], [], None, ()
    for c, (first, size) in enumerate(own_chunks):
        pieces = OWN_PIECES[min(c, len(OWN_PIECES) - 1)]
        keep, send, group, keeps = open_weights(
            place, both, gate_w, up_w, down_w, masks, keeps, first, size, tile, granule, pieces, deps
        )
        groups.append(group)
        own_sums.append(sum_of(keep, swap_cores(send), pieces, ()))
        own_others.append(from_chips(own_sums[-1]))
        deps = (own_sums[-1],)

    x_all, xt_all, og_all, tok = all_tokens(place, both, far, deps)
    deps = (tok,)
    far_sums, far_others, own_parts, waiting = [], [], [], None

    def open_own(c, deps):
        *mine, tok = pointwise(own_sums[c], own_others[c], deps)
        own_parts.append((mine, swap_cores(mine)))
        return (tok,)

    for first, size in far_chunks:
        g, offset = group_of(first)
        keep, send, tok = forward(x_all, og_all, own, *groups[g], offset * tile, size * tile, FAR_PIECES, deps)
        deps = (tok,)
        if waiting is not None:
            far_sums.append(sum_of(*waiting, FAR_PIECES, far_sums[-1:]))
            far_others.append(from_chips(far_sums[-1]))
            deps += (far_sums[-1],)
        waiting = (keep, swap_cores(send))
        if len(own_parts) < len(own_chunks) and len(far_sums) >= OWN_AFTER[len(own_parts)]:
            deps = open_own(len(own_parts), deps)
    far_sums.append(sum_of(*waiting, FAR_PIECES, far_sums[-1:]))
    far_others.append(from_chips(far_sums[-1]))

    deps = (far_sums[-1],)
    while len(own_parts) < len(own_chunks):
        deps = open_own(len(own_parts), deps)

    grads, gt, pending = None, None, []

    def flush(grads, works, deps):
        first, _, g, offset, parts, _ = works[0]
        total = sum(work[1] for work in works)
        parts, maps, begins = list(parts[:2]), [(offset, offset, offset + total - 1)] * 2, []
        for work in works:
            begins.append(work[0] - first)
            parts += work[4][2:]
            maps += [(first - work[0], 0, work[1] - 1)] * 2
        *grads, tok = weight_grads(
            grads, xt_all, og_all, *keeps, first, parts, maps, begins, first, total, tile, units, granule, deps
        )
        return grads, (tok,)

    for c, (first, size) in enumerate(far_chunks):
        g, offset = group_of(first)
        *mine, tok = pointwise(far_sums[c], far_others[c], deps)
        deps = (tok,)
        parts = (*own_parts[g], mine, swap_cores(mine))
        last = c == len(far_chunks) - 1
        if pending and not (last and DEFER):
            grads, deps = flush(grads, [pending.pop(0)], deps)
        offsets = (offset * tile, offset * tile, 0, 0)
        gt, *rest, tok = grad_tokens_of(
            gt, *groups[g][:2], offset * tile, parts, offsets, size * tile, own if last else 0, deps
        )
        deps = (tok,)
        pending.append((first, size, g, offset, parts, (offset, offset, 0, 0)))
    if len({work[2] for work in pending}) == 1:
        pending = [pending]
    else:
        pending = [[work] for work in pending]
    for works in pending:
        grads, deps = flush(grads, works, deps)

    if n_row == 4:
        arrived = [flipped(gt[(d - 1) * own : d * own], d) for d in range(1, n_row)]
    else:
        blocks = jnp.concatenate([rest[0].astype(BF), gt], axis=0).reshape(n_row, own, feats)
        wanted = [rank_row ^ b for b in range(n_row)]
        by_row = jnp.concatenate([lax.dynamic_slice_in_dim(blocks, w, 1, 0) for w in wanted], axis=0)
        arrived = [lax.psum_scatter(by_row.reshape(n_row * own, feats), "row", scatter_dimension=0, tiled=True)]
        rest = [jnp.zeros_like(rest[0])]
    return (finish(place, rest[0], arrived), *grads)


def solution(mesh):
    in_specs = (
        P(("groups", "row"), "col"),
        P(("groups", "row"), "col"),
        P(("groups", "col"), "row"),
        P(("groups", "col"), "row"),
        P(("groups", "row"), "col"),
        P("groups", None),
        P("groups", None),
        P("groups", None),
    )
    out_specs = (
        P(("groups", "row"), "col"),
        P(("groups", "col"), "row"),
        P(("groups", "col"), "row"),
        P(("groups", "row"), "col"),
    )
    step = functools.partial(local, mesh.shape["row"], mesh.shape["col"])
    return jax.shard_map(step, mesh=mesh, in_specs=in_specs, out_specs=out_specs, check_vma=False)
```
